256 devices in a mesh: group: 2 (over core), ep: 128 (over x, y, z).
Axes of the slice: x: 4, y: 4, z: 8, core: 2. Of those that a mesh axis runs over, the one named last changes fastest.
Arguments:
- thinker_rows: bfloat16 [16384, 2048], P('ep', 'group'), may hold values from -6 to 6
- owner_map: int32 [16384, 1], P('ep'), may hold values from 0 to 127, as said below
- talker_ids: int32 [16384, 8], P('ep'), may hold values from 0 to 127, all different within a row; in each aligned block of 128 rows (0 to 127, 128 to 255, ...) at most 12 rows name the same one
- project_weight: bfloat16 [2048, 1024], P('group'), may hold values from -0.125 to 0.125
- router_weight: bfloat16 [1024, 128], replicated, may hold values from -0.1875 to 0.1875
- expert_gate: bfloat16 [128, 1024, 384], P('ep'), may hold values from -0.1875 to 0.1875
- expert_up: bfloat16 [128, 1024, 384], P('ep'), may hold values from -0.1875 to 0.1875
- expert_down: bfloat16 [128, 384, 1024], P('ep'), may hold values from -0.3125 to 0.3125
Outputs:
- talker_out: bfloat16 [16384, 1024], P('ep', 'group')
The draws below stay inside these ranges and needn't reach their ends.
Inputs may be any that keep to these rules, and one draw needn't show every extreme that they name: `owner_map`: of the 128 rows of one ep index, exactly 1 have each owner. `talker_ids`: each slot names 8 different experts; in each aligned block of 128 slots (one owner's) no expert is named more than 12 times, and in some block some expert is named exactly 12 times.
All inputs are finite; a program needn't handle non-finite values.
Results may differ from the reference program's by a relative error of at most 0.0057.
Values may be sent and summed in bfloat16 or wider, within the bound.
No kernel may reach another device: no remote copies, remote signals or barrier semaphores. Data moves between devices by JAX's collectives and lax.ppermute only.
A program may use at most 64 MiB of HBM per device.

```python
import math
import jax
import jax.numpy as jnp
import numpy as np
from jax import lax

D = 2048
DT = 1024
FT = 384
TOPK = 8
QB = 32
ROWS = 128
NE = 128
TOKENS = 16384
CAPO = 1
S = 128
TALK = 16384
CAPT = 12
N_EP = 128


def shuffled_owners(source_key):
    return jax.random.permutation(source_key, ROWS) // CAPO


def draw_owner_map(key, part):
    key = jax.random.fold_in(key, 11)
    source_keys = jax.random.split(key, TOKENS // ROWS)
    owners = jax.vmap(shuffled_owners)(source_keys)
    return owners.reshape(TOKENS, 1).astype(jnp.int32)


def block_levels(stream_key, dims, pieces, low, high):
    gain = 1.0
    for axis_at, parts in pieces:
        heights = jax.random.uniform(jax.random.fold_in(jax.random.fold_in(stream_key, 6), axis_at), (parts,), jnp.float32, low / len(pieces), high / len(pieces))
        gain = gain * jnp.repeat(jnp.exp(heights), dims[axis_at] // parts).reshape((-1,) + (1,) * (len(dims) - 1 - axis_at))
    return gain


def assign_block(stream_key, own, number, rows, number_of, top, reach, slope):
    sequence = jax.random.permutation(stream_key, number_of)
    crowded, usual = portions_of(number_of, rows * top, reach, slope, True), portions_of(number_of, rows * top, reach, slope, False)
    places = jnp.arange(number_of)

    def named(lengths, turn):
        used = int((lengths > 0).sum())
        fixed = max(1, used // 4)
        shifted = fixed + (places - fixed + turn * (used - fixed)) % max(1, number_of - fixed)
        return jnp.zeros((number_of,), jnp.int32).at[sequence[jnp.where(places < fixed, places, shifted)]].set(jnp.asarray(lengths, jnp.int32))

    lengths = jnp.where(number % 4 == 0, named(crowded, number // 4), named(usual, number - number // 4 - 1))
    mixed = jax.random.permutation(jax.random.fold_in(own, 3), number_of)
    giver, taker = mixed[0:number_of // 2 * 2:2], mixed[1:number_of // 2 * 2:2]
    margin = jnp.minimum(lengths[giver] - 1, reach - lengths[taker]) // 2
    margin = jnp.where((giver == sequence[0]) | (taker == sequence[0]) | (lengths[taker] == 0), 0, jnp.maximum(margin, 0))
    shifted = jax.random.randint(jax.random.fold_in(own, 4), (number_of // 2,), 0, 1 << 20) % (margin + 1)
    lengths = lengths.at[giver].add(-shifted).at[taker].add(shifted)
    labels = jnp.searchsorted(jnp.cumsum(lengths), jnp.arange(rows * top), side="right").astype(jnp.int32)
    table = labels.reshape(top, rows).T
    table = table[jax.random.permutation(jax.random.fold_in(own, 1), rows)]
    turn = jax.random.randint(jax.random.fold_in(own, 2), (rows, 1), 0, top)
    return jnp.take_along_axis(table, (jnp.arange(top)[None, :] + turn) % top, axis=1)


def portions_of(number_of, total, reach, lean, full):
    portions = [(1 << 20) // math.isqrt(grade ** lean) + 1 for grade in range(1, number_of + 1)]
    largest = reach if full else min(reach, max(-(-total // number_of), total * portions[0] // sum(portions)))
    least = 1 if total - largest >= number_of - 1 else 0
    counts, spare = [largest] + [least] * (number_of - 1), total - largest - least * (number_of - 1)
    while spare > 0:
        movable = [i for i in range(1, number_of) if counts[i] < largest] or [i for i in range(1, number_of) if counts[i] < reach]
        mass, budget = sum([portions[i] for i in movable]), spare
        for i in movable:
            addition = min(reach - counts[i], max(1, budget * portions[i] // mass), spare)
            counts[i] = counts[i] + addition
            spare = spare - addition
    return np.array(counts)


def gaussian(stream_key, dims, width, reach, cuts=(), kind=jnp.bfloat16):
    level = block_levels(stream_key, dims, cuts, -0.22, 0.18) if cuts else 1.0
    array = jax.random.normal(stream_key, dims, jnp.float32) * width * level
    return jnp.minimum(jnp.maximum(array, -reach), reach).astype(kind)


def setup_inputs(seed: int = 0) -> dict:
    seeds = jax.random.split(jax.random.key(seed), 9)
    thinker_rows = gaussian(seeds[0], (TOKENS, D), 1.0, 6.0, ((0, 128), (1, 2)))
    owner_map = draw_owner_map(jax.random.fold_in(seeds[8], 71), 0)
    talker_ids_keys = jax.random.split(jax.random.fold_in(seeds[2], 1), TALK // S)
    talker_ids_turns = jax.random.permutation(jax.random.fold_in(seeds[2], 3), TALK // S)
    talker_ids = jax.vmap(lambda own, number: assign_block(jax.random.fold_in(seeds[2], 2), own, number, S, NE, TOPK, CAPT, 2))(talker_ids_keys, talker_ids_turns).reshape((TALK, TOPK))
    project_weight = gaussian(seeds[3], (D, DT), D ** -0.5, 0.125, ((0, 2),))
    router_weight = gaussian(seeds[4], (DT, NE), DT ** -0.5, 0.1875)
    expert_gate = gaussian(seeds[5], (NE, DT, FT), DT ** -0.5, 0.1875, ((0, 128),))
    expert_up = gaussian(seeds[6], (NE, DT, FT), DT ** -0.5, 0.1875, ((0, 128),))
    expert_down = gaussian(seeds[7], (NE, FT, DT), FT ** -0.5, 0.3125, ((0, 128),))
    return {"thinker_rows": thinker_rows, "owner_map": owner_map, "talker_ids": talker_ids, "project_weight": project_weight, "router_weight": router_weight, "expert_gate": expert_gate, "expert_up": expert_up, "expert_down": expert_down}


def block_quantize(values):
    row_total, feature_total = values.shape
    blocks = values.astype(jnp.float32).reshape(row_total, feature_total // QB, QB)
    largest = lax.optimization_barrier(jnp.max(jnp.abs(blocks), axis=2))
    scales = jnp.full(largest.shape, 16.0, jnp.float32)
    for exponent in range(3, -31, -1):
        scales = jnp.where(448.0 * 2.0 ** exponent >= largest, 2.0 ** exponent, scales)
    ratios = blocks / scales[:, :, None]
    magnitude = jnp.abs(ratios)
    spacing = jnp.full(ratios.shape, 2.0 ** (-9), jnp.float32)
    for exponent in range(-6, 9):
        spacing = jnp.where(magnitude >= 2.0 ** exponent, 2.0 ** (exponent - 3), spacing)
    scaled = (jnp.floor(ratios / spacing + 0.5) * spacing).astype(jnp.bfloat16)
    return (scaled, scales.astype(jnp.bfloat16))

def dequantize(scaled, scales):
    row_total = scaled.shape[0]
    restored = scaled.astype(jnp.float32) * scales.astype(jnp.float32)[:, :, None]
    return restored.astype(jnp.bfloat16).reshape(row_total, -1)

def slot_positions(targets, target_count):
    onehot = (targets[:, None] == jnp.arange(target_count, dtype=jnp.int32)[None, :]).astype(jnp.int32)
    before = jnp.cumsum(onehot, axis=0) - onehot
    return lax.optimization_barrier(jnp.sum(before * onehot, axis=1)).astype(jnp.int32)

def reference(thinker_rows, owner_map, talker_ids, project_weight, router_weight, expert_gate, expert_up, expert_down):
    scaled, scales = block_quantize(thinker_rows)
    restored = dequantize(scaled, scales)
    projected = jnp.dot(restored, project_weight, preferred_element_type=jnp.float32).astype(jnp.bfloat16)
    owners = owner_map[:, 0].reshape(N_EP, ROWS)
    slot_ranks = jax.vmap(lambda target: slot_positions(target, N_EP))(owners)
    sources = jnp.arange(N_EP, dtype=jnp.int32)[:, None]
    places = (owners * S + sources * CAPO + slot_ranks).reshape(-1).astype(jnp.int32)
    talker_rows = jnp.zeros((TALK, DT), jnp.bfloat16).at[places].set(projected)
    gate_float = expert_gate.astype(jnp.float32)
    up_float = expert_up.astype(jnp.float32)
    down_float = expert_down.astype(jnp.float32)

    def owner_block(inputs):
        owner_rows, chosen = inputs
        talker_float = owner_rows.astype(jnp.float32)
        inverse = lax.rsqrt(lax.optimization_barrier(jnp.mean(talker_float * talker_float, axis=1, keepdims=True)) + 1e-06)
        normed = (talker_float * inverse).astype(jnp.bfloat16)
        logits = jnp.dot(normed, router_weight, preferred_element_type=jnp.float32)
        picked_logits = jnp.take_along_axis(logits, chosen, axis=1)
        weights = jnp.exp(picked_logits)
        slot_gates = weights / lax.optimization_barrier(jnp.sum(weights, axis=1, keepdims=True))
        flat_ids = chosen.reshape(-1)
        positions = (flat_ids * CAPT + slot_positions(flat_ids, NE)).astype(jnp.int32)
        inverse_map = jnp.full((NE * CAPT,), S * TOPK, jnp.int32).at[positions].set(jnp.arange(S * TOPK, dtype=jnp.int32))
        padded = jnp.concatenate([normed, jnp.zeros((1, DT), jnp.bfloat16)], axis=0)
        gathered = jnp.take(padded, inverse_map // TOPK, axis=0).reshape(NE, CAPT, DT).astype(jnp.float32)
        gate_part = jnp.einsum('ecd,edf->ecf', gathered, gate_float)
        up_part = jnp.einsum('ecd,edf->ecf', gathered, up_float)
        hidden = (jax.nn.silu(gate_part) * up_part).astype(jnp.bfloat16)
        expert_out = jnp.einsum('ecf,efd->ecd', hidden.astype(jnp.float32), down_float).astype(jnp.bfloat16).reshape(NE * CAPT, DT)
        returned = jnp.take(expert_out, positions, axis=0).astype(jnp.float32).reshape(S, TOPK, DT)
        mixed_rows = lax.optimization_barrier(jnp.sum(slot_gates[:, :, None] * returned, axis=1))
        return (talker_float + mixed_rows).astype(jnp.bfloat16)
    result = lax.map(owner_block, (talker_rows.reshape(N_EP, S, DT), talker_ids.reshape(N_EP, S, TOPK)))
    return result.reshape(TALK, DT)
```

```python
import jax
import jax.numpy as jnp
from jax import lax
from jax.experimental import pallas as pl
from jax.experimental.pallas import tpu as pltpu
from jax.sharding import Mesh
from jax.sharding import PartitionSpec as P

F32 = jnp.float32
BF16 = jnp.bfloat16
I32 = jnp.int32
EP = ("x", "y", "zp", "zb")
REGION = ("x", "y", "zb")
SWAP = [(0, 1), (1, 0)]
SMEM = pl.BlockSpec(memory_space=pltpu.SMEM)
VMEM = pl.BlockSpec(memory_space=pltpu.VMEM)
ANY = pl.BlockSpec(memory_space=pl.ANY)
PARAMS = pltpu.CompilerParams(vmem_limit_bytes=40 * 1024 * 1024)


def iota(shape, dim):
    return lax.broadcasted_iota(I32, shape, dim)


def dot(a, b):
    return jnp.dot(a, b, preferred_element_type=F32)


def dot_nt(a, b):
    return lax.dot_general(a, b, (((1,), (1,)), ((), ())), preferred_element_type=F32)


def dot_tn(a, b):
    return lax.dot_general(a, b, (((0,), (0,)), ((), ())), preferred_element_type=F32)


def quantize(x):
    magnitude = jnp.abs(x)
    lane = iota(x.shape, 1)
    largest = magnitude
    for step in (1, 2, 4, 8, 16):
        before = pltpu.roll(largest, step, 1)
        after = pltpu.roll(largest, 128 - step, 1)
        largest = jnp.maximum(largest, jnp.where((lane & step) != 0, before, after))
    power = jnp.full(x.shape, 2.0**-31, F32)
    inverse = jnp.full(x.shape, 2.0**31, F32)
    for step in (32, 16, 8, 4, 2, 1):
        larger = power * 2.0**step
        below = larger * 448.0 < largest
        power = jnp.where(below, larger, power)
        inverse = jnp.where(below, inverse * 2.0**-step, inverse)
    scale = jnp.minimum(power * 2.0, 16.0)
    inverse = jnp.maximum(inverse * 0.5, 0.0625)
    level = scale * 2.0**-6
    inverse = inverse * 2.0**6
    for step in (8, 4, 2, 1):
        larger = level * 2.0**step
        reached = larger <= magnitude
        level = jnp.where(reached, larger, level)
        inverse = jnp.where(reached, inverse * 2.0**-step, inverse)
    return (jnp.floor(x * (inverse * 8.0) + 0.5) * (level * 0.125)).astype(BF16)


def project_kernel(place_ref, x_ref, w_hbm, keep_ref, give_ref, restored, weight, sem):
    core = place_ref[0]
    copy = pltpu.make_async_copy(w_hbm, weight, sem)
    copy.start()
    for block in range(8):
        lanes = pl.ds(block * 128, 128)
        restored[:, lanes] = quantize(x_ref[:, lanes].astype(F32))
    copy.wait()
    rows = restored[...]
    mine = pl.ds(pl.multiple_of(core * 512, 512), 512)
    other = pl.ds(pl.multiple_of((1 - core) * 512, 512), 512)
    give_ref[...] = dot(rows, weight[:, other])
    keep_ref[...] = dot(rows, weight[:, mine])


def spread_kernel(owner_ref, keep_ref, got_ref, out_ref):
    projected = (keep_ref[...] + got_ref[...]).astype(BF16)
    n = iota((128, 512), 1)
    e = n >> 2
    wanted = ((((e >> 3) << 2) + (n & 3)) << 1) + (e & 1)
    chosen = (owner_ref[...] == wanted).astype(BF16)
    rows = dot_tn(chosen, projected).astype(BF16)
    a = iota((256, 256), 0)
    b = iota((256, 256), 1)
    order = (b == ((((a >> 2) & 3) << 6) + ((a >> 4) << 2) + (a & 3))).astype(BF16)
    for g in range(8):
        part = rows[g * 64 : (g + 1) * 64]
        stack = jnp.concatenate([part[:, f * 128 : (f + 1) * 128] for f in range(4)], axis=0)
        out_ref[pl.ds(g * 256, 256), :] = dot(order, stack).astype(BF16)


def region_expert(n24, zp):
    return ((n24 >> 1) << 3) + zp * 2 + (n24 & 1)


def expand_matrix(zp):
    n = iota((768, 128), 0)
    e = (n * 2731) >> 16
    return (iota((768, 128), 1) == region_expert(e, zp)).astype(BF16)


def item_code(n, core):
    r = n - ((n * 2731) >> 16) * 24
    member = (r * 43) >> 8
    return (r - member * 6 + core * 6 + member * 16).astype(F32)


def index_kernel(place_ref, ids0, ids1, ids2, ids3, code_ref, pick_ref):
    core = place_ref[0]
    zp = place_ref[1]
    lane = iota((128, 128), 1)
    earlier = (lane < iota((128, 128), 0)).astype(BF16)
    expand = expand_matrix(zp)
    wanted = item_code(iota((768, 128), 0), core)
    for k, ids in enumerate((ids0, ids1, ids2, ids3)):
        member = (zp + 4 - k) & 3
        rows = pl.ds(pl.multiple_of(member * 128, 128), 128)
        named = lane == ids[:, 0:1]
        for t in range(1, 8):
            named = named | (lane == ids[:, t : t + 1])
        rank = dot(earlier, named.astype(F32).astype(BF16))
        code = jnp.where(named, rank + (member * 16).astype(F32), -1.0)
        code_ref[rows, :] = code
        found = dot_nt(expand, code.astype(BF16))
        pick_ref[:, rows] = (found == wanted).astype(F32).astype(BF16)


def dispatch_kernel(place_ref, own_ref, other_ref, pick_ref, send_ref, normed_ref, rest_ref, rows):
    core = place_ref[0]
    zp = place_ref[1]
    a = iota((256, 256), 0)
    b = iota((256, 256), 1)
    order = (b == (((a & 15) << 4) + (a >> 4))).astype(BF16)
    for ref, half in ((own_ref, core), (other_ref, 1 - core)):
        for g in range(8):
            part = dot(order, ref[pl.ds(g * 256, 256), :]).astype(BF16)
            for f in range(4):
                lanes = pl.ds(pl.multiple_of(half * 512 + f * 128, 128), 128)
                for member in range(4):
                    at = (f * 4 + member) * 16
                    rows[pl.ds(member * 128 + g * 16, 16), lanes] = part[at : at + 16]
    for member in range(4):
        at = pl.ds(member * 128, 128)
        value = rows[at, :].astype(F32)
        inverse = lax.rsqrt(jnp.mean(value * value, axis=1, keepdims=True) + 1e-06)
        normed_ref[at, :] = (value * inverse).astype(BF16)
    for part in range(4):
        at = pl.ds(part * 192, 192)
        send_ref[at, :] = dot(pick_ref[at, :], normed_ref[...]).astype(BF16)
    rest_ref[...] = rows[
        pl.ds(pl.multiple_of(zp * 128, 128), 128), pl.ds(pl.multiple_of(core * 512, 512), 512)
    ]


def gate_kernel(place_ref, normed_ref, router_ref, code_ref, mix_ref):
    core = place_ref[0]
    zp = place_ref[1]
    expand = expand_matrix(zp)
    wanted = item_code(iota((128, 768), 1), core)
    for member in range(4):
        at = pl.ds(member * 128, 128)
        code = code_ref[at, :]
        logits = dot(normed_ref[at, :], router_ref[...])
        weights = jnp.where(code >= 0.0, jnp.exp(logits), 0.0)
        gates = weights / jnp.sum(weights, axis=1, keepdims=True)
        found = dot_nt(code.astype(BF16), expand)
        spread = dot_nt(gates.astype(BF16), expand)
        mix_ref[at, :] = jnp.where(found == wanted, spread, 0.0).astype(BF16)


def expert_kernel(x_ref, gate_ref, up_ref, down_ref, out_ref):
    x = x_ref[...]
    gate = dot(x, gate_ref[0])
    up = dot(x, up_ref[0])
    hidden = (gate / (1.0 + jnp.exp(-gate)) * up).astype(BF16)
    out_ref[...] = dot(hidden, down_ref[0]).astype(BF16)


def mix_kernel(mine, place_ref, mix_ref, back_ref, out_ref):
    core = place_ref[0]
    half = core if mine else 1 - core
    lanes = pl.ds(pl.multiple_of(half * 512, 512), 512)
    out_ref[...] = dot(mix_ref[...], back_ref[:, lanes]).astype(out_ref.dtype)


def share_kernel(place_ref, keep_ref, got_ref, own_ref, one_ref, two_ref, three_ref):
    zp = place_ref[1]
    for k, ref in enumerate((own_ref, one_ref, two_ref, three_ref)):
        at = pl.ds(pl.multiple_of(((zp + k) & 3) * 128, 128), 128)
        ref[...] = (keep_ref[at, :] + got_ref[at, :].astype(F32)).astype(ref.dtype)


def call(kernel, outs, ins, scratch=(), specs=None):
    return pl.pallas_call(
        kernel,
        out_shape=[jax.ShapeDtypeStruct(shape, dtype) for shape, dtype in outs],
        in_specs=specs or [SMEM] + [VMEM] * (len(ins) - 1),
        out_specs=[VMEM] * len(outs),
        scratch_shapes=list(scratch),
        compiler_params=PARAMS,
    )(*ins)


def around(k):
    return [(i, (i + k) % 4) for i in range(4)]


def body(
    thinker_rows,
    owner_map,
    talker_ids,
    project_weight,
    router_weight,
    expert_gate,
    expert_up,
    expert_down,
):
    core = lax.axis_index("group")
    zp = lax.axis_index("zp")
    place = jnp.stack([core, zp]).astype(I32)
    keep, give = call(
        project_kernel,
        [((128, 512), F32)] * 2,
        (place, thinker_rows, project_weight),
        [pltpu.VMEM((128, 1024), BF16), pltpu.VMEM((1024, 1024), BF16), pltpu.SemaphoreType.DMA],
        [SMEM, VMEM, ANY],
    )
    got = lax.ppermute(give, "group", SWAP)
    (sent,) = call(
        spread_kernel, [((2048, 128), BF16)], (owner_map, keep, got), specs=[VMEM, VMEM, VMEM]
    )
    own = lax.all_to_all(sent.reshape(128, 16, 128), EP, 0, 0, tiled=True)
    ids = [talker_ids] + [lax.ppermute(talker_ids, "zp", around(k)) for k in (1, 2, 3)]
    code, pick = call(
        index_kernel, [((512, 128), F32), ((768, 512), BF16)], (place, *ids)
    )
    other = lax.ppermute(own, "group", SWAP)
    send, normed, rest = call(
        dispatch_kernel,
        [((768, 1024), BF16), ((512, 1024), BF16), ((128, 512), BF16)],
        (place, own.reshape(2048, 128), other.reshape(2048, 128), pick),
        [pltpu.VMEM((512, 1024), BF16)],
    )
    items = lax.all_to_all(send.reshape(32, 24, 1024), REGION, 0, 0, tiled=True)
    (mix,) = call(gate_kernel, [((512, 768), BF16)], (place, normed, router_weight, code))
    expert_out = pl.pallas_call(
        expert_kernel,
        grid=(4,),
        out_shape=jax.ShapeDtypeStruct((768, 1024), BF16),
        in_specs=[
            pl.BlockSpec((192, 1024), lambda i: (i, 0)),
            pl.BlockSpec((1, 1024, 384), lambda i: (0, 0, 0)),
            pl.BlockSpec((1, 1024, 384), lambda i: (0, 0, 0)),
            pl.BlockSpec((1, 384, 1024), lambda i: (0, 0, 0)),
        ],
        out_specs=pl.BlockSpec((192, 1024), lambda i: (i, 0)),
        compiler_params=PARAMS,
    )(items.reshape(768, 1024), expert_gate, expert_up, expert_down)
    back = lax.all_to_all(expert_out.reshape(32, 24, 1024), REGION, 0, 0, tiled=True)
    back = back.reshape(768, 1024)

    def mixed(mine, dtype):
        return call(
            lambda *refs: mix_kernel(mine, *refs), [((512, 512), dtype)], (place, mix, back)
        )[0]

    given = lax.ppermute(mixed(False, F32), "group", SWAP)
    kept = mixed(True, F32)
    own_part, one, two, three = call(
        share_kernel, [((128, 512), F32)] + [((128, 512), BF16)] * 3, (place, kept, given)
    )
    total = own_part
    for k, part in ((1, one), (2, two), (3, three)):
        total = total + lax.ppermute(part, "zp", around(k)).astype(F32)
    return (rest.astype(F32) + total).astype(BF16)


def solution(mesh):
    ep = ("x", "y", "zp", "zb")
    split = Mesh(mesh.devices.reshape(2, 4, 4, 4, 2), ("group",) + ep)
    return jax.shard_map(
        body,
        mesh=split,
        in_specs=(
            P(ep, "group"),
            P(ep, None),
            P(ep, None),
            P("group", None),
            P(),
            P(ep, None, None),
            P(ep, None, None),
            P(ep, None, None),
        ),
        out_specs=P(ep, "group"),
        check_vma=False,
    )
```

```python
import jax
import jax.numpy as jnp
from jax import lax
from jax.experimental import pallas as pl
from jax.experimental.pallas import tpu as pltpu
from jax.sharding import Mesh
from jax.sharding import PartitionSpec as P

F32 = jnp.float32
BF16 = jnp.bfloat16
I32 = jnp.int32
EP = ("x", "y", "zp", "zb")
REGION = ("x", "y", "zb")
SWAP = [(0, 1), (1, 0)]
SMEM = pl.BlockSpec(memory_space=pltpu.SMEM)
VMEM = pl.BlockSpec(memory_space=pltpu.VMEM)
HBM = pl.BlockSpec(memory_space=pltpu.HBM)
PARAMS = pltpu.CompilerParams(vmem_limit_bytes=40 * 1024 * 1024)


def iota(shape, dim):
    return lax.broadcasted_iota(I32, shape, dim)


def dot(a, b):
    return jnp.dot(a, b, preferred_element_type=F32)


def dot_nt(a, b):
    return lax.dot_general(a, b, (((1,), (1,)), ((), ())), preferred_element_type=F32)


def dot_tn(a, b):
    return lax.dot_general(a, b, (((0,), (0,)), ((), ())), preferred_element_type=F32)


def quantize(x):
    magnitude = jnp.abs(x)
    lane = iota(x.shape, 1)
    largest = magnitude
    for step in (1, 2, 4, 8, 16):
        before = pltpu.roll(largest, step, 1)
        after = pltpu.roll(largest, 128 - step, 1)
        largest = jnp.maximum(largest, jnp.where((lane & step) != 0, before, after))
    power = jnp.full(x.shape, 2.0**-31, F32)
    inverse = jnp.full(x.shape, 2.0**31, F32)
    for step in (32, 16, 8, 4, 2, 1):
        larger = power * 2.0**step
        below = larger * 448.0 < largest
        power = jnp.where(below, larger, power)
        inverse = jnp.where(below, inverse * 2.0**-step, inverse)
    scale = jnp.minimum(power * 2.0, 16.0)
    inverse = jnp.maximum(inverse * 0.5, 0.0625)
    level = scale * 2.0**-6
    inverse = inverse * 2.0**6
    for step in (8, 4, 2, 1):
        larger = level * 2.0**step
        reached = larger <= magnitude
        level = jnp.where(reached, larger, level)
        inverse = jnp.where(reached, inverse * 2.0**-step, inverse)
    return (jnp.floor(x * (inverse * 8.0) + 0.5) * (level * 0.125)).astype(BF16)


def project_kernel(place_ref, x_ref, w_hbm, keep_ref, give_ref, restored, weight, sem):
    core = place_ref[0]
    copy = pltpu.make_async_copy(w_hbm, weight, sem)
    copy.start()
    for block in range(8):
        lanes = pl.ds(block * 128, 128)
        restored[:, lanes] = quantize(x_ref[:, lanes].astype(F32))
    copy.wait()
    rows = restored[...]
    mine = pl.ds(pl.multiple_of(core * 512, 512), 512)
    other = pl.ds(pl.multiple_of((1 - core) * 512, 512), 512)
    give_ref[...] = dot(rows, weight[:, other])
    keep_ref[...] = dot(rows, weight[:, mine])


def by24(n):
    return (n * 2731) >> 16


def spread_kernel(owner_ref, keep_ref, got_ref, ids_ref, out_ref):
    projected = (keep_ref[...] + got_ref[...]).astype(BF16)
    n = iota((128, 512), 1)
    e = n >> 2
    wanted = ((((e >> 3) << 2) + (n & 3)) << 1) + (e & 1)
    chosen = (owner_ref[...] == wanted).astype(BF16)
    rows = dot_tn(chosen, projected).astype(BF16)
    pad = (iota((16, 8), 0) == iota((16, 8), 1)).astype(BF16)
    ids = dot_nt(pad, ids_ref[...].astype(F32).astype(BF16)).astype(BF16)
    a = iota((192, 144), 0)
    e = by24(a)
    i = a - e * 24
    source = jnp.where(i < 16, ((i >> 2) << 5) + (e << 2) + (i & 3), 112 + i)
    order = (iota((192, 144), 1) == source).astype(BF16)
    for g in range(16):
        part = rows[g * 32 : (g + 1) * 32]
        stack = jnp.concatenate([part[:, f * 128 : (f + 1) * 128] for f in range(4)] + [ids], axis=0)
        out_ref[pl.ds(g * 192, 192), :] = dot(order, stack).astype(BF16)


def expand_matrix(zp):
    e = by24(iota((768, 128), 0))
    return (iota((768, 128), 1) == ((e >> 1) << 3) + zp * 2 + (e & 1)).astype(BF16)


def item_code(n, half):
    r = n - by24(n) * 24
    member = (r * 43) >> 8
    return (r - member * 6 + half * 6 + member * 16).astype(F32)


def index_kernel(place_ref, own_ref, code_ref, pick_ref):
    core, zp, xy, zb = (place_ref[i] for i in range(4))
    expert = iota((128, 128), 0)
    earlier = (expert < iota((128, 128), 1)).astype(BF16)
    expert = expert.astype(F32)
    expand = expand_matrix(zp)
    wanted = item_code(iota((768, 128), 0), core)
    a = iota((16, 48), 0)
    choose = ((iota((16, 48), 1) == zb * 24 + 16 + a) & (a < 8)).astype(F32).astype(BF16)
    for member in range(4):
        pair = pl.ds(pl.multiple_of((xy * 4 + member) * 48, 48), 48)
        ids = dot(choose, own_ref[pair, :])
        named = expert == ids[0:1, :]
        for t in range(1, 8):
            named = named | (expert == ids[t : t + 1, :])
        rank = dot(named.astype(F32).astype(BF16), earlier)
        code = jnp.where(named, rank + 16.0 * member, -1.0)
        code_ref[pl.ds(member * 128, 128), :] = code.T
        found = dot(expand, code.astype(BF16))
        pick_ref[:, pl.ds(member * 128, 128)] = (found == wanted).astype(F32).astype(BF16)


def dispatch_kernel(place_ref, own_ref, other_ref, pick_ref, send_ref, normed_ref, rest_ref, rows):
    core = place_ref[0]
    zp = place_ref[1]
    a = iota((256, 384), 0)
    b = iota((256, 384), 1)
    order = (b == (a & 15) * 24 + (a >> 4)).astype(BF16)
    for ref, half in ((own_ref, core), (other_ref, 1 - core)):
        for g in range(8):
            part = dot(order, ref[pl.ds(g * 384, 384), :]).astype(BF16)
            for f in range(4):
                lanes = pl.ds(pl.multiple_of(half * 512 + f * 128, 128), 128)
                for member in range(4):
                    at = (f * 4 + member) * 16
                    rows[pl.ds(member * 128 + g * 16, 16), lanes] = part[at : at + 16]
    for member in range(4):
        at = pl.ds(member * 128, 128)
        value = rows[at, :].astype(F32)
        inverse = lax.rsqrt(jnp.mean(value * value, axis=1, keepdims=True) + 1e-06)
        normed_ref[at, :] = (value * inverse).astype(BF16)
    for part in range(4):
        at = pl.ds(part * 192, 192)
        send_ref[at, :] = dot(pick_ref[at, :], normed_ref[...]).astype(BF16)
    rest_ref[...] = rows[
        pl.ds(pl.multiple_of(zp * 128, 128), 128), pl.ds(pl.multiple_of(core * 512, 512), 512)
    ]


def gate_kernel(place_ref, normed_ref, router_ref, code_ref, mix0_ref, mix1_ref):
    expand = expand_matrix(place_ref[1])
    wanted = [item_code(iota((128, 768), 1), half) for half in (0, 1)]
    for member in range(4):
        at = pl.ds(member * 128, 128)
        code = code_ref[at, :]
        logits = dot(normed_ref[at, :], router_ref[...])
        weights = jnp.where(code >= 0.0, jnp.exp(logits), 0.0)
        gates = weights / jnp.sum(weights, axis=1, keepdims=True)
        found = dot_nt(code.astype(BF16), expand)
        spread = dot_nt(gates.astype(BF16), expand)
        mix0_ref[at, :] = jnp.where(found == wanted[0], spread, 0.0).astype(BF16)
        mix1_ref[at, :] = jnp.where(found == wanted[1], spread, 0.0).astype(BF16)


def hidden_kernel(x_ref, gate_ref, up_ref, out_ref):
    x = x_ref[...]
    gate = dot(x, gate_ref[0])
    up = dot(x, up_ref[0])
    out_ref[...] = (gate / (1.0 + jnp.exp(-gate)) * up).astype(BF16)


def down_kernel(place_ref, own_ref, other_ref, down_ref, out_ref):
    core = place_ref[0]
    mine = pl.ds(pl.multiple_of(core * 512, 512), 512)
    other = pl.ds(pl.multiple_of((1 - core) * 512, 512), 512)
    weight = down_ref[0, :, mine]
    out_ref[:, mine] = dot(own_ref[...], weight).astype(BF16)
    out_ref[:, other] = dot(other_ref[...], weight).astype(BF16)


def mix_kernel(place_ref, mix0_ref, mix1_ref, back_ref, rest_ref, own_ref, one_ref, two_ref, three_ref):
    zp = place_ref[1]
    for k, ref in ((2, two_ref), (1, one_ref), (3, three_ref), (0, own_ref)):
        at = pl.ds(pl.multiple_of(((zp + k) & 3) * 128, 128), 128)
        total = dot(mix0_ref[at, :], back_ref[:, 0:512]) + dot(mix1_ref[at, :], back_ref[:, 512:1024])
        if k == 0:
            total = total + rest_ref[...].astype(F32)
        ref[...] = total.astype(ref.dtype)


def call(kernel, outs, ins, scratch=(), specs=None):
    return pl.pallas_call(
        kernel,
        out_shape=[jax.ShapeDtypeStruct(shape, dtype) for shape, dtype in outs],
        in_specs=specs or [SMEM] + [VMEM] * (len(ins) - 1),
        out_specs=[VMEM] * len(outs),
        scratch_shapes=list(scratch),
        compiler_params=PARAMS,
    )(*ins)


def around(k):
    return [(i, (i + k) % 4) for i in range(4)]


def body(
    thinker_rows,
    owner_map,
    talker_ids,
    project_weight,
    router_weight,
    expert_gate,
    expert_up,
    expert_down,
):
    core = lax.axis_index("group")
    zp = lax.axis_index("zp")
    place = jnp.stack([core, zp, lax.axis_index(("x", "y")), lax.axis_index("zb")]).astype(I32)
    keep, give = call(
        project_kernel,
        [((128, 512), F32)] * 2,
        (place, thinker_rows, project_weight),
        [pltpu.VMEM((128, 1024), BF16), pltpu.VMEM((1024, 1024), BF16), pltpu.SemaphoreType.DMA],
        [SMEM, VMEM, HBM],
    )
    got = lax.ppermute(give, "group", SWAP)
    (sent,) = call(
        spread_kernel,
        [((3072, 128), BF16)],
        (owner_map, keep, got, talker_ids),
        specs=[VMEM] * 4,
    )
    own = lax.all_to_all(sent.reshape(128, 24, 128), EP, 0, 0, tiled=True)
    other = lax.ppermute(own, "group", SWAP)
    code, pick = call(
        index_kernel,
        [((512, 128), F32), ((768, 512), BF16)],
        (place, own.reshape(3072, 128)),
    )
    send, normed, rest = call(
        dispatch_kernel,
        [((768, 1024), BF16), ((512, 1024), BF16), ((128, 512), BF16)],
        (place, own.reshape(3072, 128), other.reshape(3072, 128), pick),
        [pltpu.VMEM((512, 1024), BF16)],
    )
    items = lax.all_to_all(send.reshape(32, 24, 1024), REGION, 0, 0, tiled=True)
    mix0, mix1 = call(
        gate_kernel, [((512, 768), BF16)] * 2, (place, normed, router_weight, code)
    )
    hidden = pl.pallas_call(
        hidden_kernel,
        grid=(4,),
        out_shape=jax.ShapeDtypeStruct((768, 384), BF16),
        in_specs=[
            pl.BlockSpec((192, 1024), lambda i: (i, 0)),
            pl.BlockSpec((1, 1024, 384), lambda i: (0, 0, 0)),
            pl.BlockSpec((1, 1024, 384), lambda i: (0, 0, 0)),
        ],
        out_specs=pl.BlockSpec((192, 384), lambda i: (i, 0)),
        compiler_params=PARAMS,
    )(items.reshape(768, 1024), expert_gate, expert_up)
    other_hidden = lax.ppermute(hidden, "group", SWAP)
    (expert_out,) = call(
        down_kernel, [((768, 1024), BF16)], (place, hidden, other_hidden, expert_down)
    )
    back = lax.all_to_all(expert_out.reshape(32, 24, 1024), REGION, 0, 0, tiled=True)
    total, one, two, three = call(
        mix_kernel,
        [((128, 512), F32)] + [((128, 512), BF16)] * 3,
        (place, mix0, mix1, back.reshape(768, 1024), rest),
    )
    for k, part in ((2, two), (1, one), (3, three)):
        total = total + lax.ppermute(part, "zp", around(k)).astype(F32)
    return total.astype(BF16)


def solution(mesh):
    ep = ("x", "y", "zp", "zb")
    split = Mesh(mesh.devices.reshape(2, 4, 4, 4, 2), ("group",) + ep)
    return jax.shard_map(
        body,
        mesh=split,
        in_specs=(
            P(ep, "group"),
            P(ep, None),
            P(ep, None),
            P("group", None),
            P(),
            P(ep, None, None),
            P(ep, None, None),
            P(ep, None, None),
        ),
        out_specs=P(ep, "group"),
        check_vma=False,
    )
```

```python
import functools

import jax
import jax.numpy as jnp
from jax import lax
from jax.experimental import pallas as pl
from jax.experimental.pallas import tpu as pltpu
from jax.sharding import Mesh
from jax.sharding import PartitionSpec as P

F32 = jnp.float32
BF16 = jnp.bfloat16
I32 = jnp.int32
EP = ("x", "y", "zp", "zb")
REGION = ("x", "y", "zb")
SWAP = [(0, 1), (1, 0)]
VMEM = pl.BlockSpec(memory_space=pltpu.VMEM)
HBM = pl.BlockSpec(memory_space=pltpu.HBM)
PARAMS = pltpu.CompilerParams(vmem_limit_bytes=16 * 1024 * 1024)


def iota(shape, dim):
    return lax.broadcasted_iota(I32, shape, dim)


def dot(a, b):
    return jnp.dot(a, b, preferred_element_type=F32)


def dot_nt(a, b):
    return lax.dot_general(a, b, (((1,), (1,)), ((), ())), preferred_element_type=F32)


def dot_tn(a, b):
    return lax.dot_general(a, b, (((0,), (0,)), ((), ())), preferred_element_type=F32)


def quantize(x_ref, out_ref):
    rows = x_ref.shape[0]
    r = iota((128, 128), 0)
    lane = iota((128, 128), 1)
    compact = jnp.zeros((rows, 128), F32)
    for b in range(8):
        largest = jnp.abs(x_ref[:, pl.ds(b * 128, 128)].astype(F32))
        for step in (16, 8, 4, 2, 1):
            largest = jnp.maximum(largest, pltpu.roll(largest, 128 - step, 1))
        first = (lane == r + b) & ((r & 31) == 0)
        compact = compact + dot(largest.astype(BF16), first.astype(F32).astype(BF16))
    power = jnp.full(compact.shape, 2.0**-31, F32)
    inverse = jnp.full(compact.shape, 2.0**31, F32)
    for step in (32, 16, 8, 4, 2, 1):
        larger = power * 2.0**step
        below = larger * 448.0 < compact
        power = jnp.where(below, larger, power)
        inverse = jnp.where(below, inverse * 2.0**-step, inverse)
    spacing = (jnp.minimum(power * 2.0, 16.0) * 2.0**-9).astype(BF16)
    inverse = (jnp.maximum(inverse * 0.5, 0.0625) * 2.0**9).astype(BF16)
    for b in range(8):
        lanes = pl.ds(b * 128, 128)
        spread = (r == (lane & 96) + b).astype(F32).astype(BF16)
        x = x_ref[:, lanes].astype(F32)
        size = jnp.abs(x) * 0.125
        level = dot(spacing, spread)
        over = dot(inverse, spread)
        for step in (8, 4, 2, 1):
            larger = level * 2.0**step
            reached = larger <= size
            level = jnp.where(reached, larger, level)
            over = jnp.where(reached, over * 2.0**-step, over)
        out_ref[:, lanes] = (jnp.floor(x * over + 0.5) * level).astype(BF16)


def halves():
    core = lax.axis_index("group")
    mine = pl.ds(pl.multiple_of(core * 512, 512), 512)
    other = pl.ds(pl.multiple_of((1 - core) * 512, 512), 512)
    return mine, other


def project_kernel(x_ref, w_hbm, give_ref, keep_ref, restored, weight, sem):
    copy = pltpu.make_async_copy(w_hbm, weight, sem)
    copy.start()
    quantize(x_ref, restored)
    copy.wait()
    mine, other = halves()
    give_ref[...] = dot(restored[...], weight[:, other])
    keep_ref[...] = dot(restored[...], weight[:, mine])


def by24(n):
    return (n * 2731) >> 16


def spread_kernel(owner_ref, keep_ref, got_ref, ids_ref, out_ref):
    projected = (keep_ref[...] + got_ref[...]).astype(BF16)
    n = iota((128, 512), 1)
    e = n >> 2
    wanted = ((((e >> 3) << 2) + (n & 3)) << 1) + (e & 1)
    chosen = (owner_ref[...] == wanted).astype(BF16)
    rows = dot_tn(chosen, projected).astype(BF16)
    pad = (iota((16, 8), 0) == iota((16, 8), 1)).astype(BF16)
    ids = dot_nt(pad, ids_ref[...].astype(F32).astype(BF16)).astype(BF16)
    a = iota((192, 144), 0)
    e = by24(a)
    i = a - e * 24
    source = jnp.where(i < 16, ((i >> 2) << 5) + (e << 2) + (i & 3), 112 + i)
    order = (iota((192, 144), 1) == source).astype(BF16)
    for g in range(16):
        part = rows[g * 32 : (g + 1) * 32]
        stack = jnp.concatenate([part[:, f * 128 : (f + 1) * 128] for f in range(4)] + [ids], axis=0)
        out_ref[pl.ds(g * 192, 192), :] = dot(order, stack).astype(BF16)


def expand_matrix(zp):
    e = by24(iota((768, 128), 0))
    return (iota((768, 128), 1) == ((e >> 1) << 3) + zp * 2 + (e & 1)).astype(BF16)


def item_code(n, half):
    r = n - by24(n) * 24
    member = (r * 43) >> 8
    return (r - member * 6 + half * 6 + member * 16).astype(F32)


def index_kernel(own_ref, code_ref, pick_ref):
    core, zp, xy, zb = (lax.axis_index(name) for name in ("group", "zp", ("x", "y"), "zb"))
    expert = iota((128, 128), 0)
    earlier = (expert < iota((128, 128), 1)).astype(BF16)
    expert = expert.astype(F32)
    expand = expand_matrix(zp)
    wanted = item_code(iota((768, 128), 0), core)
    a = iota((16, 48), 0)
    choose = ((iota((16, 48), 1) == zb * 24 + 16 + a) & (a < 8)).astype(F32).astype(BF16)
    for member in range(4):
        pair = pl.ds(pl.multiple_of((xy * 4 + member) * 48, 48), 48)
        ids = dot(choose, own_ref[pair, :])
        named = expert == ids[0:1, :]
        for t in range(1, 8):
            named = named | (expert == ids[t : t + 1, :])
        rank = dot(named.astype(F32).astype(BF16), earlier)
        code = jnp.where(named, rank + 16.0 * member, -1.0)
        code_ref[pl.ds(member * 128, 128), :] = code.T
        found = dot(expand, code.astype(BF16))
        pick_ref[:, pl.ds(member * 128, 128)] = (found == wanted).astype(F32).astype(BF16)


def dispatch_kernel(own_ref, other_ref, pick_ref, send_ref, normed_ref, rest_ref, rows):
    core = lax.axis_index("group")
    zp = lax.axis_index("zp")
    a = iota((256, 384), 0)
    b = iota((256, 384), 1)
    order = (b == (a & 15) * 24 + (a >> 4)).astype(BF16)
    for ref, half in ((own_ref, core), (other_ref, 1 - core)):
        for g in range(8):
            part = dot(order, ref[pl.ds(g * 384, 384), :]).astype(BF16)
            for f in range(4):
                lanes = pl.ds(pl.multiple_of(half * 512 + f * 128, 128), 128)
                for member in range(4):
                    at = (f * 4 + member) * 16
                    rows[pl.ds(member * 128 + g * 16, 16), lanes] = part[at : at + 16]
    for member in range(4):
        at = pl.ds(member * 128, 128)
        value = rows[at, :].astype(F32)
        inverse = lax.rsqrt(jnp.mean(value * value, axis=1, keepdims=True) + 1e-06)
        normed_ref[at, :] = (value * inverse).astype(BF16)
    for part in range(4):
        at = pl.ds(part * 192, 192)
        send_ref[at, :] = dot(pick_ref[at, :], normed_ref[...]).astype(BF16)
    rest_ref[...] = rows[
        pl.ds(pl.multiple_of(zp * 128, 128), 128), pl.ds(pl.multiple_of(core * 512, 512), 512)
    ]


def gate_kernel(normed_ref, router_ref, code_ref, mix0_ref, mix1_ref):
    expand = expand_matrix(lax.axis_index("zp"))
    wanted = [item_code(iota((128, 768), 1), half) for half in (0, 1)]
    for member in range(4):
        at = pl.ds(member * 128, 128)
        code = code_ref[at, :]
        logits = dot(normed_ref[at, :], router_ref[...])
        weights = jnp.where(code >= 0.0, jnp.exp(logits), 0.0)
        gates = weights / jnp.sum(weights, axis=1, keepdims=True)
        found = dot_nt(code.astype(BF16), expand)
        spread = dot_nt(gates.astype(BF16), expand)
        mix0_ref[at, :] = jnp.where(found == wanted[0], spread, 0.0).astype(BF16)
        mix1_ref[at, :] = jnp.where(found == wanted[1], spread, 0.0).astype(BF16)


def hidden_kernel(x_ref, gate_ref, up_ref, out_ref):
    for i in range(3):
        at = pl.ds(i * 256, 256)
        x = x_ref[at, :]
        gate = dot(x, gate_ref[0])
        up = dot(x, up_ref[0])
        out_ref[at, :] = (gate / (1.0 + jnp.exp(-gate)) * up).astype(BF16)


def down_kernel(whose, hidden_ref, down_ref, *refs):
    out_hbm, stage, sems = refs[-3:]
    pair = halves()
    copies = []
    for i in range(3):
        at = pl.ds(i * 256, 256)
        stage[at, :] = dot(hidden_ref[at, :], down_ref[0, :, pair[0]]).astype(BF16)
        copies.append(
            pltpu.make_async_copy(stage.at[at, :], out_hbm.at[at, pair[whose]], sems.at[i])
        )
        copies[-1].start()
    for copy in copies:
        copy.wait()


def mix_kernel(
    mix0_ref, mix1_hbm, back_ref, rest_ref, two_ref, one_ref, three_ref, own_ref, mix1, total, sem
):
    zp = lax.axis_index("zp")
    copy = pltpu.make_async_copy(mix1_hbm, mix1, sem)
    copy.start()
    total[...] = dot(mix0_ref[...], back_ref[:, 0:512])
    copy.wait()
    for k, ref in ((2, two_ref), (1, one_ref), (3, three_ref), (0, own_ref)):
        at = pl.ds(pl.multiple_of(((zp + k) & 3) * 128, 128), 128)
        value = total[at, :] + dot(mix1[at, :], back_ref[:, 512:1024])
        if k == 0:
            value = value + rest_ref[...].astype(F32)
        ref[...] = value.astype(ref.dtype)


def call(kernel, outs, ins, scratch=(), specs=None, out_spec=VMEM, aliases=None):
    return pl.pallas_call(
        kernel,
        out_shape=[jax.ShapeDtypeStruct(shape, dtype) for shape, dtype in outs],
        in_specs=specs or [VMEM] * len(ins),
        out_specs=[out_spec] * len(outs),
        scratch_shapes=list(scratch),
        input_output_aliases=aliases or {},
        compiler_params=PARAMS,
    )(*ins)


def pinned(x):
    return pltpu.with_memory_space_constraint(x, pltpu.HBM)


def around(k):
    return [(i, (i + k) % 4) for i in range(4)]


def body(
    thinker_rows,
    owner_map,
    talker_ids,
    project_weight,
    router_weight,
    expert_gate,
    expert_up,
    expert_down,
):
    give, keep = call(
        project_kernel,
        [((128, 512), F32)] * 2,
        (pinned(thinker_rows), pinned(project_weight)),
        [pltpu.VMEM((128, 1024), BF16), pltpu.VMEM((1024, 1024), BF16), pltpu.SemaphoreType.DMA],
        [VMEM, HBM],
    )
    got = lax.ppermute(give, "group", SWAP)
    (sent,) = call(spread_kernel, [((3072, 128), BF16)], (owner_map, keep, got, talker_ids))
    own = lax.all_to_all(sent.reshape(128, 24, 128), EP, 0, 0, tiled=True)
    other = lax.ppermute(own, "group", SWAP)
    code, pick = call(
        index_kernel, [((512, 128), F32), ((768, 512), BF16)], (own.reshape(3072, 128),)
    )
    send, normed, rest = call(
        dispatch_kernel,
        [((768, 1024), BF16), ((512, 1024), BF16), ((128, 512), BF16)],
        (own.reshape(3072, 128), other.reshape(3072, 128), pick),
        [pltpu.VMEM((512, 1024), BF16)],
    )
    items = lax.all_to_all(send.reshape(32, 24, 1024), REGION, 0, 0, tiled=True)
    mix0, mix1 = call(gate_kernel, [((512, 768), BF16)] * 2, (normed, router_weight, code))
    (hidden,) = call(
        hidden_kernel,
        [((768, 384), BF16)],
        (items.reshape(768, 1024), expert_gate, expert_up),
    )
    other_hidden = lax.ppermute(hidden, "group", SWAP)
    down = functools.partial(
        call,
        outs=[((768, 1024), BF16)],
        scratch=[pltpu.VMEM((768, 512), BF16), pltpu.SemaphoreType.DMA((3,))],
        out_spec=HBM,
    )
    (expert_out,) = down(functools.partial(down_kernel, 0), ins=(hidden, expert_down))
    (expert_out,) = down(
        functools.partial(down_kernel, 1),
        ins=(other_hidden, expert_down, expert_out),
        specs=[VMEM, VMEM, HBM],
        aliases={2: 0},
    )
    back = lax.all_to_all(expert_out.reshape(32, 24, 1024), REGION, 0, 0, tiled=True)
    two, one, three, total = call(
        mix_kernel,
        [((128, 512), BF16)] * 3 + [((128, 512), F32)],
        (mix0, pinned(mix1), back.reshape(768, 1024), rest),
        [pltpu.VMEM((512, 768), BF16), pltpu.VMEM((512, 512), F32), pltpu.SemaphoreType.DMA],
        [VMEM, HBM, VMEM, VMEM],
    )
    for k, part in ((2, two), (1, one), (3, three)):
        total = total + lax.ppermute(part, "zp", around(k)).astype(F32)
    return total.astype(BF16)


def solution(mesh):
    ep = ("x", "y", "zp", "zb")
    split = Mesh(mesh.devices.reshape(2, 4, 4, 4, 2), ("group",) + ep)
    return jax.shard_map(
        body,
        mesh=split,
        in_specs=(
            P(ep, "group"),
            P(ep, None),
            P(ep, None),
            P("group", None),
            P(),
            P(ep, None, None),
            P(ep, None, None),
            P(ep, None, None),
        ),
        out_specs=P(ep, "group"),
        check_vma=False,
    )
```

```python
import functools

import jax
import jax.numpy as jnp
from jax import lax
from jax.experimental import pallas as pl
from jax.experimental.pallas import tpu as pltpu
from jax.sharding import Mesh
from jax.sharding import PartitionSpec as P

F32 = jnp.float32
BF16 = jnp.bfloat16
I32 = jnp.int32
EP = ("x", "y", "zp", "zb")
REGION = ("x", "y", "zb")
SWAP = [(0, 1), (1, 0)]
VMEM = pl.BlockSpec(memory_space=pltpu.VMEM)
HBM = pl.BlockSpec(memory_space=pltpu.HBM)
PARAMS = pltpu.CompilerParams(vmem_limit_bytes=16 * 1024 * 1024)


def iota(shape, dim):
    return lax.broadcasted_iota(I32, shape, dim)


def dot(a, b):
    return jnp.dot(a, b, preferred_element_type=F32)


def dot_nt(a, b):
    return lax.dot_general(a, b, (((1,), (1,)), ((), ())), preferred_element_type=F32)


def dot_tn(a, b):
    return lax.dot_general(a, b, (((0,), (0,)), ((), ())), preferred_element_type=F32)


def quantize(x_ref, out_ref):
    rows = x_ref.shape[0]
    r = iota((128, 128), 0)
    lane = iota((128, 128), 1)
    compact = jnp.zeros((rows, 128), F32)
    for b in range(8):
        largest = jnp.abs(x_ref[:, pl.ds(b * 128, 128)].astype(F32))
        for step in (16, 8, 4, 2, 1):
            largest = jnp.maximum(largest, pltpu.roll(largest, 128 - step, 1))
        first = (lane == r + b) & ((r & 31) == 0)
        compact = compact + dot(largest.astype(BF16), first.astype(F32).astype(BF16))
    power = jnp.full(compact.shape, 2.0**-31, F32)
    inverse = jnp.full(compact.shape, 2.0**31, F32)
    for step in (32, 16, 8, 4, 2, 1):
        larger = power * 2.0**step
        below = larger * 448.0 < compact
        power = jnp.where(below, larger, power)
        inverse = jnp.where(below, inverse * 2.0**-step, inverse)
    spacing = (jnp.minimum(power * 2.0, 16.0) * 2.0**-9).astype(BF16)
    inverse = (jnp.maximum(inverse * 0.5, 0.0625) * 2.0**9).astype(BF16)
    for b in range(8):
        lanes = pl.ds(b * 128, 128)
        spread = (r == (lane & 96) + b).astype(F32).astype(BF16)
        x = x_ref[:, lanes].astype(F32)
        size = jnp.abs(x) * 0.125
        level = dot(spacing, spread)
        over = dot(inverse, spread)
        for step in (8, 4, 2, 1):
            larger = level * 2.0**step
            reached = larger <= size
            level = jnp.where(reached, larger, level)
            over = jnp.where(reached, over * 2.0**-step, over)
        out_ref[:, lanes] = (jnp.floor(x * over + 0.5) * level).astype(BF16)


def halves():
    core = lax.axis_index("group")
    mine = pl.ds(pl.multiple_of(core * 512, 512), 512)
    other = pl.ds(pl.multiple_of((1 - core) * 512, 512), 512)
    return mine, other


def project_kernel(x_ref, w_hbm, give_ref, keep_ref, restored, weight, sem):
    copy = pltpu.make_async_copy(w_hbm, weight, sem)
    copy.start()
    quantize(x_ref, restored)
    copy.wait()
    mine, other = halves()
    give_ref[...] = dot(restored[...], weight[:, other])
    keep_ref[...] = dot(restored[...], weight[:, mine])


def by24(n):
    return (n * 2731) >> 16


def prepare_kernel(owner_ref, ids_ref, chosen_ref, ids_out_ref, order_ref):
    n = iota((128, 512), 1)
    e = n >> 2
    wanted = ((((e >> 3) << 2) + (n & 3)) << 1) + (e & 1)
    chosen_ref[...] = (owner_ref[...] == wanted).astype(F32).T.astype(BF16)
    a = iota((16, 8), 0)
    part = (iota((16, 8), 1) == a + lax.axis_index("group") * 4) & (a < 4)
    ids = dot_nt(part.astype(F32).astype(BF16), ids_ref[...].astype(F32).astype(BF16))
    ids_out_ref[...] = ids.astype(BF16)
    a = iota((160, 144), 0)
    e = (a * 3277) >> 16
    i = a - e * 20
    source = jnp.where(i < 16, ((i >> 2) << 5) + (e << 2) + (i & 3), 112 + i)
    order_ref[...] = (iota((160, 144), 1) == source).astype(F32).astype(BF16)


def spread_kernel(keep_ref, got_ref, chosen_ref, ids_ref, order_ref, out_ref):
    projected = (keep_ref[...] + got_ref[...]).astype(BF16)
    rows = dot(chosen_ref[...], projected).astype(BF16)
    ids = ids_ref[...]
    order = order_ref[...]
    for g in range(16):
        part = rows[g * 32 : (g + 1) * 32]
        stack = jnp.concatenate([part[:, f * 128 : (f + 1) * 128] for f in range(4)] + [ids], axis=0)
        out_ref[pl.ds(g * 160, 160), :] = dot(order, stack).astype(BF16)


def expand_matrix(zp):
    e = by24(iota((768, 128), 0))
    return (iota((768, 128), 1) == ((e >> 1) << 3) + zp * 2 + (e & 1)).astype(BF16)


def item_code(n, half):
    r = n - by24(n) * 24
    member = (r * 43) >> 8
    return (r - member * 6 + half * 6 + member * 16).astype(F32)


def arrange(ref, rows, at, order):
    for g in range(8):
        part = dot(order, ref[pl.ds(g * 320, 320), :]).astype(BF16)
        for f in range(4):
            lanes = pl.ds(pl.multiple_of(at + f * 128, 128), 128)
            for member in range(4):
                first = (f * 4 + member) * 16
                rows[pl.ds(member * 128 + g * 16, 16), lanes] = part[first : first + 16]


def arrange_kernel(own_ref, rows_ref, order_ref, expand_ref):
    a = iota((256, 320), 0)
    order = (iota((256, 320), 1) == (a & 15) * 20 + (a >> 4)).astype(F32).astype(BF16)
    order_ref[...] = order
    expand_ref[:, 0:128] = expand_matrix(lax.axis_index("zp"))
    taken = item_code(iota((768, 128), 0), lax.axis_index("group"))
    expand_ref[:, 128:256] = jnp.where(iota((768, 128), 1) == 0, -taken, 0.0).astype(BF16)
    arrange(own_ref, rows_ref, 0, order)


def find_items(own_ref, other_ref, expand_ref, code_ref, pick):
    xy, zb = lax.axis_index(("x", "y")), lax.axis_index("zb")
    expert = iota((128, 128), 0)
    earlier = (expert < iota((128, 128), 1)).astype(F32).astype(BF16)
    expert = expert.astype(F32)
    a = iota((16, 160), 0)
    line = pl.ds(pl.multiple_of(xy * 160, 160), 160)
    choose = (iota((16, 160), 1) == (a >> 2) * 40 + zb * 20 + 16 + (a & 3)).astype(F32).astype(BF16)
    first = dot(choose, own_ref[line, :])
    second = dot(choose, other_ref[line, :])
    expand = expand_ref[...]
    ones = jnp.ones((128, 128), BF16)
    for member in range(4):
        named = expert == first[member * 4 : member * 4 + 1, :]
        for t in range(1, 4):
            named = named | (expert == first[member * 4 + t : member * 4 + t + 1, :])
        for t in range(4):
            named = named | (expert == second[member * 4 + t : member * 4 + t + 1, :])
        rank = dot(named.astype(F32).astype(BF16), earlier)
        code = jnp.where(named, rank + 16.0 * member, -1.0)
        code_ref[pl.ds(member * 128, 128), 1024:1152] = code.T.astype(BF16)
        found = dot(expand, jnp.concatenate([code.astype(BF16), ones], axis=0))
        pick[:, pl.ds(member * 128, 128)] = (found == 0.0).astype(F32).astype(BF16)


def dispatch_kernel(
    own_ref, other_ref, mine_ref, order_ref, expand_ref, send_ref, normed_ref, rows, pick
):
    zp = lax.axis_index("zp")
    mine, other = halves()
    find_items(own_ref, other_ref, expand_ref, normed_ref, pick)
    rows[:, mine] = mine_ref[...]
    arrange(other_ref, rows, (1 - lax.axis_index("group")) * 512, order_ref[...])
    for member in range(4):
        at = pl.ds(member * 128, 128)
        value = rows[at, :].astype(F32)
        inverse = lax.rsqrt(jnp.mean(value * value, axis=1, keepdims=True) + 1e-06)
        normed_ref[at, 0:1024] = (value * inverse).astype(BF16)
    for part in range(2):
        at = pl.ds(part * 384, 384)
        send_ref[at, :] = dot(pick[at, :], normed_ref[0:512, 0:1024]).astype(BF16)
    normed_ref[512:640, 0:512] = mine_ref[pl.ds(pl.multiple_of(zp * 128, 128), 128), :]


def gate_kernel(normed_ref, router_ref, mix_ref):
    mix_ref[512:640, 0:512] = normed_ref[512:640, 0:512]
    expand = expand_matrix(lax.axis_index("zp"))
    wanted = [item_code(iota((128, 768), 1), half) for half in (0, 1)]
    for member in range(4):
        at = pl.ds(member * 128, 128)
        code = normed_ref[at, 1024:1152]
        logits = dot(normed_ref[at, 0:1024], router_ref[...])
        weights = jnp.where(code.astype(F32) >= 0.0, jnp.exp(logits), 0.0)
        gates = weights / jnp.sum(weights, axis=1, keepdims=True)
        found = dot_nt(code, expand)
        spread = dot_nt(gates.astype(BF16), expand)
        mix_ref[at, 0:768] = jnp.where(found == wanted[0], spread, 0.0).astype(BF16)
        mix_ref[at, 768:1536] = jnp.where(found == wanted[1], spread, 0.0).astype(BF16)


def hidden_kernel(x_ref, gate_ref, up_ref, out_ref):
    x = x_ref[...]

    def act(gate, up):
        return (gate / (1.0 + jnp.exp(-gate)) * up).astype(BF16)

    out_ref[:, 0:256] = act(dot(x, gate_ref[0, :, 0:256]), dot(x, up_ref[0, :, 0:256]))
    last = jnp.concatenate([gate_ref[0, :, 256:384], up_ref[0, :, 256:384]], axis=1)
    both = dot(x, last)
    out_ref[:, 256:384] = act(both[:, 0:128], both[:, 128:256])


def down_kernel(whose, hidden_ref, down_ref, *refs):
    out_hbm, stage, sems = refs[-3:]
    pair = halves()
    copies = []
    for i in range(2):
        at = pl.ds(i * 384, 384)
        stage[at, :] = dot(hidden_ref[at, :], down_ref[0, :, pair[0]]).astype(BF16)
        for j in range(2):
            at = pl.ds(i * 384 + j * 192, 192)
            copies.append(
                pltpu.make_async_copy(
                    stage.at[at, :], out_hbm.at[at, pair[whose]], sems.at[i * 2 + j]
                )
            )
            copies[-1].start()
    for copy in copies:
        copy.wait()


def mix_kernel(mix_ref, back_ref, two_ref, one_ref, three_ref, own_ref, total):
    zp = lax.axis_index("zp")
    items = jnp.concatenate([back_ref[:, 0:512], back_ref[:, 512:1024]], axis=0)
    total[...] = dot(mix_ref[0:512, :], items)
    for k, ref in ((2, two_ref), (1, one_ref), (3, three_ref), (0, own_ref)):
        value = total[pl.ds(pl.multiple_of(((zp + k) & 3) * 128, 128), 128), :]
        if k == 0:
            value = value + mix_ref[512:640, 0:512].astype(F32)
        ref[...] = value.astype(ref.dtype)


def call(kernel, outs, ins, scratch=(), specs=None, out_spec=VMEM, aliases=None):
    return pl.pallas_call(
        kernel,
        out_shape=[jax.ShapeDtypeStruct(shape, dtype) for shape, dtype in outs],
        in_specs=specs or [VMEM] * len(ins),
        out_specs=[out_spec] * len(outs),
        scratch_shapes=list(scratch),
        input_output_aliases=aliases or {},
        compiler_params=PARAMS,
    )(*ins)


def pinned(x):
    return pltpu.with_memory_space_constraint(x, pltpu.HBM)


def around(k):
    return [(i, (i + k) % 4) for i in range(4)]


def body(
    thinker_rows,
    owner_map,
    talker_ids,
    project_weight,
    router_weight,
    expert_gate,
    expert_up,
    expert_down,
):
    give, keep = call(
        project_kernel,
        [((128, 512), F32)] * 2,
        (pinned(thinker_rows), pinned(project_weight)),
        [pltpu.VMEM((128, 1024), BF16), pltpu.VMEM((1024, 1024), BF16), pltpu.SemaphoreType.DMA],
        [VMEM, HBM],
    )
    got = lax.ppermute(give, "group", SWAP)
    chosen, ids, order = call(
        prepare_kernel,
        [((512, 128), BF16), ((16, 128), BF16), ((160, 144), BF16)],
        (owner_map, talker_ids),
    )
    (sent,) = call(spread_kernel, [((2560, 128), BF16)], (keep, got, chosen, ids, order))
    own = lax.all_to_all(sent.reshape(128, 5, 4, 128), EP, 0, 0, tiled=True)
    other = lax.ppermute(own, "group", SWAP).reshape(2560, 128)
    own = own.reshape(2560, 128)
    mine, order, expand = call(
        arrange_kernel,
        [((512, 512), BF16), ((256, 320), BF16), ((768, 256), BF16)],
        (own,),
    )
    send, normed = call(
        dispatch_kernel,
        [((768, 1024), BF16), ((640, 1152), BF16)],
        (own, other, mine, order, expand),
        [pltpu.VMEM((512, 1024), BF16), pltpu.VMEM((768, 512), BF16)],
    )
    items = lax.all_to_all(send.reshape(32, 24, 1024), REGION, 0, 0, tiled=True)
    (mix,) = call(gate_kernel, [((640, 1536), BF16)], (normed, router_weight))
    (hidden,) = call(
        hidden_kernel,
        [((768, 384), BF16)],
        (items.reshape(768, 1024), expert_gate, expert_up),
    )
    other_hidden = lax.ppermute(hidden, "group", SWAP)
    down = functools.partial(
        call,
        outs=[((768, 1024), BF16)],
        scratch=[pltpu.VMEM((768, 512), BF16), pltpu.SemaphoreType.DMA((4,))],
        out_spec=HBM,
    )
    (expert_out,) = down(functools.partial(down_kernel, 0), ins=(hidden, expert_down))
    (expert_out,) = down(
        functools.partial(down_kernel, 1),
        ins=(other_hidden, expert_down, expert_out),
        specs=[VMEM, VMEM, HBM],
        aliases={2: 0},
    )
    back = lax.all_to_all(expert_out.reshape(32, 24, 1024), REGION, 0, 0, tiled=True)
    two, one, three, total = call(
        mix_kernel,
        [((128, 512), BF16)] * 3 + [((128, 512), F32)],
        (mix, back.reshape(768, 1024)),
        [pltpu.VMEM((512, 512), F32)],
    )
    for k, part in ((2, two), (1, one), (3, three)):
        total = total + lax.ppermute(part, "zp", around(k)).astype(F32)
    return total.astype(BF16)


def solution(mesh):
    ep = ("x", "y", "zp", "zb")
    split = Mesh(mesh.devices.reshape(2, 4, 4, 4, 2), ("group",) + ep)
    return jax.shard_map(
        body,
        mesh=split,
        in_specs=(
            P(ep, "group"),
            P(ep, None),
            P(ep, None),
            P("group", None),
            P(),
            P(ep, None, None),
            P(ep, None, None),
            P(ep, None, None),
        ),
        out_specs=P(ep, "group"),
        check_vma=False,
    )
```

```python
import functools

import jax
import jax.numpy as jnp
from jax import lax
from jax.experimental import pallas as pl
from jax.experimental.pallas import tpu as pltpu
from jax.sharding import PartitionSpec as P

F32 = jnp.float32
BF16 = jnp.bfloat16
I32 = jnp.int32
EP_FIRST = 112
REGION_FIRST = 21
EP = [[(r + EP_FIRST) % 128 for r in range(128)]]
REGIONS = [
    [(i >> 1) * 8 + zp * 2 + (i & 1) for i in ((r + REGION_FIRST) % 32 for r in range(32))]
    for zp in range(4)
]
SWAP = [(0, 1), (1, 0)]
VMEM = pl.BlockSpec(memory_space=pltpu.VMEM)
HBM = pl.BlockSpec(memory_space=pltpu.HBM)
PARAMS = pltpu.CompilerParams(vmem_limit_bytes=16 * 1024 * 1024)


def my_zp():
    return (lax.axis_index("ep") >> 1) & 3


def iota(shape, dim):
    return lax.broadcasted_iota(I32, shape, dim)


def dot(a, b):
    return jnp.dot(a, b, preferred_element_type=F32)


def dot_nt(a, b):
    return lax.dot_general(a, b, (((1,), (1,)), ((), ())), preferred_element_type=F32)


def dot_tn(a, b):
    return lax.dot_general(a, b, (((0,), (0,)), ((), ())), preferred_element_type=F32)


def quantize(x_ref, out_ref):
    rows = x_ref.shape[0]
    r = iota((128, 128), 0)
    lane = iota((128, 128), 1)
    compact = jnp.zeros((rows, 128), F32)
    for b in range(8):
        largest = jnp.abs(x_ref[:, pl.ds(b * 128, 128)].astype(F32))
        for step in (16, 8, 4, 2, 1):
            largest = jnp.maximum(largest, pltpu.roll(largest, 128 - step, 1))
        first = (lane == r + b) & ((r & 31) == 0)
        compact = compact + dot(largest.astype(BF16), first.astype(F32).astype(BF16))
    power = jnp.full(compact.shape, 2.0**-31, F32)
    inverse = jnp.full(compact.shape, 2.0**31, F32)
    for step in (32, 16, 8, 4, 2, 1):
        larger = power * 2.0**step
        below = larger * 448.0 < compact
        power = jnp.where(below, larger, power)
        inverse = jnp.where(below, inverse * 2.0**-step, inverse)
    spacing = (jnp.minimum(power * 2.0, 16.0) * 2.0**-9).astype(BF16)
    inverse = (jnp.maximum(inverse * 0.5, 0.0625) * 2.0**9).astype(BF16)
    for b in range(8):
        lanes = pl.ds(b * 128, 128)
        spread = (r == (lane & 96) + b).astype(F32).astype(BF16)
        x = x_ref[:, lanes].astype(F32)
        size = jnp.abs(x) * 0.125
        level = dot(spacing, spread)
        over = dot(inverse, spread)
        for step in (8, 4, 2, 1):
            larger = level * 2.0**step
            reached = larger <= size
            level = jnp.where(reached, larger, level)
            over = jnp.where(reached, over * 2.0**-step, over)
        out_ref[:, lanes] = (jnp.floor(x * over + 0.5) * level).astype(BF16)


def halves():
    core = lax.axis_index("group")
    mine = pl.ds(pl.multiple_of(core * 512, 512), 512)
    other = pl.ds(pl.multiple_of((1 - core) * 512, 512), 512)
    return mine, other


def project_kernel(x_ref, w_hbm, give_ref, keep_ref, restored, weight, sem):
    copy = pltpu.make_async_copy(w_hbm, weight, sem)
    copy.start()
    quantize(x_ref, restored)
    copy.wait()
    mine, other = halves()
    give_ref[...] = dot(restored[...], weight[:, other])
    keep_ref[...] = dot(restored[...], weight[:, mine])


def by24(n):
    return (n * 2731) >> 16


def prepare_kernel(owner_ref, ids_ref, chosen_ref, ids_out_ref, order_ref):
    n = iota((128, 512), 1)
    e = ((n >> 2) + EP_FIRST) & 127
    wanted = ((((e >> 3) << 2) + (n & 3)) << 1) + (e & 1)
    chosen_ref[...] = (owner_ref[...] == wanted).astype(F32).T.astype(BF16)
    a = iota((16, 8), 0)
    part = (iota((16, 8), 1) == a + lax.axis_index("group") * 4) & (a < 4)
    ids = dot_nt(part.astype(F32).astype(BF16), ids_ref[...].astype(F32).astype(BF16))
    ids_out_ref[...] = ids.astype(BF16)
    a = iota((160, 144), 0)
    e = (a * 3277) >> 16
    i = a - e * 20
    source = jnp.where(i < 16, ((i >> 2) << 5) + (e << 2) + (i & 3), 112 + i)
    order_ref[...] = (iota((160, 144), 1) == source).astype(F32).astype(BF16)


def spread_kernel(keep_ref, got_ref, chosen_ref, ids_ref, order_ref, out_ref):
    projected = (keep_ref[...] + got_ref[...]).astype(BF16)
    rows = dot(chosen_ref[...], projected).astype(BF16)
    ids = ids_ref[...]
    order = order_ref[...]
    for g in range(16):
        part = rows[g * 32 : (g + 1) * 32]
        stack = jnp.concatenate([part[:, f * 128 : (f + 1) * 128] for f in range(4)] + [ids], axis=0)
        out_ref[pl.ds(g * 160, 160), :] = dot(order, stack).astype(BF16)


def expand_matrix(zp):
    e = (by24(iota((768, 128), 0)) + REGION_FIRST) & 31
    return (iota((768, 128), 1) == ((e >> 1) << 3) + zp * 2 + (e & 1)).astype(BF16)


def item_code(n, half):
    r = n - by24(n) * 24
    member = (r * 43) >> 8
    return (r - member * 6 + half * 6 + member * 16).astype(F32)


def arrange(ref, rows, at, order):
    for g in range(8):
        slots = (g * 16 + EP_FIRST) % 128
        part = dot(order, ref[pl.ds(g * 320, 320), :]).astype(BF16)
        for f in range(4):
            lanes = pl.ds(pl.multiple_of(at + f * 128, 128), 128)
            for member in range(4):
                first = (f * 4 + member) * 16
                rows[pl.ds(member * 128 + slots, 16), lanes] = part[first : first + 16]


def arrange_kernel(own_ref, rows_ref, order_ref, expand_ref):
    a = iota((256, 320), 0)
    order = (iota((256, 320), 1) == (a & 15) * 20 + (a >> 4)).astype(F32).astype(BF16)
    order_ref[...] = order
    expand_ref[:, 0:128] = expand_matrix(my_zp())
    taken = item_code(iota((768, 128), 0), lax.axis_index("group"))
    expand_ref[:, 128:256] = jnp.where(iota((768, 128), 1) == 0, -taken, 0.0).astype(BF16)
    arrange(own_ref, rows_ref, 0, order)


def find_items(own_ref, other_ref, expand_ref, code_ref, pick):
    ep = lax.axis_index("ep")
    zb = ep & 1
    expert = iota((128, 128), 0)
    earlier = (expert < iota((128, 128), 1)).astype(F32).astype(BF16)
    expert = expert.astype(F32)
    a = iota((16, 160), 0)
    line = pl.ds(pl.multiple_of((((ep + 128 - EP_FIRST) & 127) >> 3) * 160, 160), 160)
    choose = (iota((16, 160), 1) == (a >> 2) * 40 + zb * 20 + 16 + (a & 3)).astype(F32).astype(BF16)
    first = dot(choose, own_ref[line, :])
    second = dot(choose, other_ref[line, :])
    expand = expand_ref[...]
    ones = jnp.ones((128, 128), BF16)
    for member in range(4):
        named = expert == first[member * 4 : member * 4 + 1, :]
        for t in range(1, 4):
            named = named | (expert == first[member * 4 + t : member * 4 + t + 1, :])
        for t in range(4):
            named = named | (expert == second[member * 4 + t : member * 4 + t + 1, :])
        rank = dot(named.astype(F32).astype(BF16), earlier)
        code = jnp.where(named, rank + 16.0 * member, -1.0)
        code_ref[pl.ds(member * 128, 128), 1024:1152] = code.T.astype(BF16)
        found = dot(expand, jnp.concatenate([code.astype(BF16), ones], axis=0))
        pick[:, pl.ds(member * 128, 128)] = (found == 0.0).astype(F32).astype(BF16)


def dispatch_kernel(
    own_ref, other_ref, mine_ref, order_ref, expand_ref, send_ref, normed_ref, rows, pick
):
    zp = my_zp()
    mine, other = halves()
    find_items(own_ref, other_ref, expand_ref, normed_ref, pick)
    rows[:, mine] = mine_ref[...]
    arrange(other_ref, rows, (1 - lax.axis_index("group")) * 512, order_ref[...])
    for member in range(4):
        at = pl.ds(member * 128, 128)
        value = rows[at, :].astype(F32)
        inverse = lax.rsqrt(jnp.mean(value * value, axis=1, keepdims=True) + 1e-06)
        normed_ref[at, 0:1024] = (value * inverse).astype(BF16)
    for part in range(2):
        at = pl.ds(part * 384, 384)
        send_ref[at, :] = dot(pick[at, :], normed_ref[0:512, 0:1024]).astype(BF16)
    normed_ref[512:640, 0:512] = mine_ref[pl.ds(pl.multiple_of(zp * 128, 128), 128), :]


def gate_kernel(normed_ref, router_ref, mix_ref):
    mix_ref[512:640, 0:512] = normed_ref[512:640, 0:512]
    expand = expand_matrix(my_zp())
    wanted = [item_code(iota((128, 768), 1), half) for half in (0, 1)]
    for member in range(4):
        at = pl.ds(member * 128, 128)
        code = normed_ref[at, 1024:1152]
        logits = dot(normed_ref[at, 0:1024], router_ref[...])
        weights = jnp.where(code.astype(F32) >= 0.0, jnp.exp(logits), 0.0)
        gates = weights / jnp.sum(weights, axis=1, keepdims=True)
        found = dot_nt(code, expand)
        spread = dot_nt(gates.astype(BF16), expand)
        mix_ref[at, 0:768] = jnp.where(found == wanted[0], spread, 0.0).astype(BF16)
        mix_ref[at, 768:1536] = jnp.where(found == wanted[1], spread, 0.0).astype(BF16)


def hidden_kernel(x_ref, gate_ref, up_ref, out_ref):
    x = x_ref[...]

    def act(gate, up):
        return (gate / (1.0 + jnp.exp(-gate)) * up).astype(BF16)

    out_ref[:, 0:256] = act(dot(x, gate_ref[0, :, 0:256]), dot(x, up_ref[0, :, 0:256]))
    last = jnp.concatenate([gate_ref[0, :, 256:384], up_ref[0, :, 256:384]], axis=1)
    both = dot(x, last)
    out_ref[:, 256:384] = act(both[:, 0:128], both[:, 128:256])


def down_kernel(whose, hidden_ref, down_ref, *refs):
    out_hbm, stage, sems = refs[-3:]
    pair = halves()
    copies = []
    for i in range(2):
        at = pl.ds(i * 384, 384)
        stage[at, :] = dot(hidden_ref[at, :], down_ref[0, :, pair[0]]).astype(BF16)
        for j in range(2):
            at = pl.ds(i * 384 + j * 192, 192)
            copies.append(
                pltpu.make_async_copy(
                    stage.at[at, :], out_hbm.at[at, pair[whose]], sems.at[i * 2 + j]
                )
            )
            copies[-1].start()
    for copy in copies:
        copy.wait()


def mix_kernel(mix_ref, back_ref, two_ref, one_ref, three_ref, own_ref, total):
    zp = my_zp()
    items = jnp.concatenate([back_ref[:, 0:512], back_ref[:, 512:1024]], axis=0)
    total[...] = dot(mix_ref[0:512, :], items)
    for k, ref in ((2, two_ref), (1, one_ref), (3, three_ref), (0, own_ref)):
        value = total[pl.ds(pl.multiple_of(((zp + k) & 3) * 128, 128), 128), :]
        if k == 0:
            value = value + mix_ref[512:640, 0:512].astype(F32)
        ref[...] = value.astype(ref.dtype)


def call(kernel, outs, ins, scratch=(), specs=None, out_spec=VMEM, aliases=None):
    return pl.pallas_call(
        kernel,
        out_shape=[jax.ShapeDtypeStruct(shape, dtype) for shape, dtype in outs],
        in_specs=specs or [VMEM] * len(ins),
        out_specs=[out_spec] * len(outs),
        scratch_shapes=list(scratch),
        input_output_aliases=aliases or {},
        compiler_params=PARAMS,
    )(*ins)


def pinned(x):
    return pltpu.with_memory_space_constraint(x, pltpu.HBM)


def around(k):
    return [(i, (i & ~7) + ((i + 2 * k) & 7)) for i in range(128)]


def exchange(x, groups):
    return lax.all_to_all(x, "ep", 0, 0, axis_index_groups=groups, tiled=True)


def body(
    thinker_rows,
    owner_map,
    talker_ids,
    project_weight,
    router_weight,
    expert_gate,
    expert_up,
    expert_down,
):
    give, keep = call(
        project_kernel,
        [((128, 512), F32)] * 2,
        (pinned(thinker_rows), pinned(project_weight)),
        [pltpu.VMEM((128, 1024), BF16), pltpu.VMEM((1024, 1024), BF16), pltpu.SemaphoreType.DMA],
        [VMEM, HBM],
    )
    got = lax.ppermute(give, "group", SWAP)
    chosen, ids, order = call(
        prepare_kernel,
        [((512, 128), BF16), ((16, 128), BF16), ((160, 144), BF16)],
        (owner_map, talker_ids),
    )
    (sent,) = call(spread_kernel, [((2560, 128), BF16)], (keep, got, chosen, ids, order))
    own = exchange(sent.reshape(128, 5, 4, 128), EP)
    other = lax.ppermute(own, "group", SWAP).reshape(2560, 128)
    own = own.reshape(2560, 128)
    mine, order, expand = call(
        arrange_kernel,
        [((512, 512), BF16), ((256, 320), BF16), ((768, 256), BF16)],
        (own,),
    )
    send, normed = call(
        dispatch_kernel,
        [((768, 1024), BF16), ((640, 1152), BF16)],
        (own, other, mine, order, expand),
        [pltpu.VMEM((512, 1024), BF16), pltpu.VMEM((768, 512), BF16)],
    )
    items = exchange(send.reshape(32, 24, 1024), REGIONS)
    (mix,) = call(gate_kernel, [((640, 1536), BF16)], (normed, router_weight))
    (hidden,) = call(
        hidden_kernel,
        [((768, 384), BF16)],
        (items.reshape(768, 1024), expert_gate, expert_up),
    )
    other_hidden = lax.ppermute(hidden, "group", SWAP)
    down = functools.partial(
        call,
        outs=[((768, 1024), BF16)],
        scratch=[pltpu.VMEM((768, 512), BF16), pltpu.SemaphoreType.DMA((4,))],
        out_spec=HBM,
    )
    (expert_out,) = down(functools.partial(down_kernel, 0), ins=(hidden, expert_down))
    (expert_out,) = down(
        functools.partial(down_kernel, 1),
        ins=(other_hidden, expert_down, expert_out),
        specs=[VMEM, VMEM, HBM],
        aliases={2: 0},
    )
    back = exchange(expert_out.reshape(32, 24, 1024), REGIONS)
    two, one, three, total = call(
        mix_kernel,
        [((128, 512), BF16)] * 3 + [((128, 512), F32)],
        (mix, back.reshape(768, 1024)),
        [pltpu.VMEM((512, 512), F32)],
    )
    for k, part in ((2, two), (1, one), (3, three)):
        total = total + lax.ppermute(part, "ep", around(k)).astype(F32)
    return total.astype(BF16)


def solution(mesh):
    return jax.shard_map(
        body,
        mesh=mesh,
        in_specs=(
            P("ep", "group"),
            P("ep", None),
            P("ep", None),
            P("group", None),
            P(),
            P("ep", None, None),
            P("ep", None, None),
            P("ep", None, None),
        ),
        out_specs=P("ep", "group"),
        check_vma=False,
    )
```

```python
import jax
import jax.numpy as jnp
from jax import lax
from jax.experimental import pallas as pl
from jax.experimental.pallas import tpu as pltpu
from jax.sharding import PartitionSpec as P

F32 = jnp.float32
BF16 = jnp.bfloat16
I32 = jnp.int32
EP_FIRST = 112
REGION_FIRST = 21
EP = [[(r + EP_FIRST) % 128 for r in range(128)]]
REGIONS = [
    [(i & 15) * 8 + zp * 2 + (i >> 4) for i in ((r + REGION_FIRST) % 32 for r in range(32))]
    for zp in range(4)
]
SWAP = [(0, 1), (1, 0)]
VMEM = pl.BlockSpec(memory_space=pltpu.VMEM)
HBM = pl.BlockSpec(memory_space=pltpu.HBM)
PARAMS = pltpu.CompilerParams(vmem_limit_bytes=16 * 1024 * 1024)


def my_zp():
    return (lax.axis_index("ep") >> 1) & 3


def iota(shape, dim):
    return lax.broadcasted_iota(I32, shape, dim)


def dot(a, b):
    return jnp.dot(a, b, preferred_element_type=F32)


def dot_nt(a, b):
    return lax.dot_general(a, b, (((1,), (1,)), ((), ())), preferred_element_type=F32)


def dot_tn(a, b):
    return lax.dot_general(a, b, (((0,), (0,)), ((), ())), preferred_element_type=F32)


def quantize(x_ref, out_ref):
    rows = x_ref.shape[0]
    r = iota((128, 128), 0)
    lane = iota((128, 128), 1)
    compact = jnp.zeros((rows, 128), F32)
    for b in range(8):
        largest = jnp.abs(x_ref[:, pl.ds(b * 128, 128)].astype(F32))
        for step in (16, 8, 4, 2, 1):
            largest = jnp.maximum(largest, pltpu.roll(largest, 128 - step, 1))
        first = (lane == r + b) & ((r & 31) == 0)
        compact = compact + dot(largest.astype(BF16), first.astype(F32).astype(BF16))
    power = jnp.full(compact.shape, 2.0**-31, F32)
    inverse = jnp.full(compact.shape, 2.0**31, F32)
    for step in (32, 16, 8, 4, 2, 1):
        larger = power * 2.0**step
        below = larger * 448.0 < compact
        power = jnp.where(below, larger, power)
        inverse = jnp.where(below, inverse * 2.0**-step, inverse)
    spacing = (jnp.minimum(power * 2.0, 16.0) * 2.0**-9).astype(BF16)
    inverse = (jnp.maximum(inverse * 0.5, 0.0625) * 2.0**9).astype(BF16)
    for b in range(8):
        lanes = pl.ds(b * 128, 128)
        spread = (r == (lane & 96) + b).astype(F32).astype(BF16)
        x = x_ref[:, lanes].astype(F32)
        size = jnp.abs(x) * 0.125
        level = dot(spacing, spread)
        over = dot(inverse, spread)
        for step in (8, 4, 2, 1):
            larger = level * 2.0**step
            reached = larger <= size
            level = jnp.where(reached, larger, level)
            over = jnp.where(reached, over * 2.0**-step, over)
        out_ref[:, lanes] = (jnp.floor(x * over + 0.5) * level).astype(BF16)


def halves():
    core = lax.axis_index("group")
    mine = pl.ds(pl.multiple_of(core * 512, 512), 512)
    other = pl.ds(pl.multiple_of((1 - core) * 512, 512), 512)
    return mine, other


def project_kernel(x_ref, owner_ref, w_hbm, give_ref, keep_ref, restored, weight, sem):
    copy = pltpu.make_async_copy(w_hbm, weight, sem)
    copy.start()
    quantize(x_ref, restored)
    core = lax.axis_index("group")
    n = iota((128, 128), 0)
    half = jnp.where(n < 64, 1 - core, core)
    owner = ((((n & 63) >> 2) * 4 + half * 2 + (n & 1)) << 1) + ((n >> 1) & 1)
    chosen = (owner_ref[...] == owner).astype(F32).astype(BF16)
    rows = dot(chosen, restored[...]).astype(BF16)
    copy.wait()
    both = dot(rows, weight[...])
    give_ref[...] = both[0:64]
    keep_ref[...] = both[64:128]


def by24(n):
    return (n * 2731) >> 16


def prepare_kernel(chosen_ref, order_ref):
    a = iota((256, 64), 0)
    e = ((a >> 1) + EP_FIRST) & 127
    chosen = iota((256, 64), 1) == (((e >> 3) << 1) + (e & 1)) * 2 + (a & 1)
    chosen_ref[...] = chosen.astype(F32).astype(BF16)
    a = iota((256, 256), 0)
    source = (((a >> 1) & 7) << 5) + ((a >> 4) << 1) + (a & 1)
    order_ref[...] = (iota((256, 256), 1) == source).astype(F32).astype(BF16)


def spread_kernel(keep_ref, got_ref, chosen_ref, order_ref, out_ref):
    projected = (keep_ref[...] + got_ref[...]).astype(BF16)
    rows = dot(chosen_ref[...], projected).astype(BF16)
    order = order_ref[...]
    for g in range(8):
        part = rows[g * 32 : (g + 1) * 32]
        stack = jnp.concatenate([part[:, f * 128 : (f + 1) * 128] for f in range(8)], axis=0)
        out_ref[pl.ds(g * 256, 256), :] = dot(order, stack).astype(BF16)


def expand_matrix(zp):
    e = (by24(iota((768, 128), 0)) + REGION_FIRST) & 31
    return (iota((768, 128), 1) == ((e & 15) << 3) + zp * 2 + (e >> 4)).astype(BF16)


def item_code(n):
    r = n - by24(n) * 24
    return jnp.where(r < 12, r, r + 4).astype(F32)


def setup_kernel(order_ref, expand_ref):
    a = iota((256, 256), 0)
    order_ref[...] = (iota((256, 256), 1) == ((a & 15) << 4) + (a >> 4)).astype(F32).astype(BF16)
    expand_ref[:, 0:128] = expand_matrix(my_zp())
    taken = item_code(iota((768, 128), 0))
    expand_ref[:, 128:256] = jnp.where(iota((768, 128), 1) == 0, -taken, 0.0).astype(BF16)


def dispatch_kernel(
    own_ref, order_ref, expand_ref, ids_ref, ids_got_ref, send_ref, normed_ref, rows, pick
):
    core = lax.axis_index("group")
    zp = my_zp()
    expert = iota((128, 128), 0)
    earlier = (expert < iota((128, 128), 1)).astype(F32).astype(BF16)
    expand = expand_ref[...]
    ones = jnp.ones((128, 128), BF16)
    for member in range(2):
        k = (zp + 4 - core * 2 - member) & 3
        ids = jnp.where(core == 1, ids_ref[k], ids_got_ref[k])
        named = expert == ids[0:1, :]
        for t in range(1, 8):
            named = named | (expert == ids[t : t + 1, :])
        rank = dot(named.astype(F32).astype(BF16), earlier)
        code = jnp.where(named, rank + 16.0 * member, -1.0)
        normed_ref[pl.ds(member * 128, 128), 1024:1152] = code.T.astype(BF16)
        found = dot(expand, jnp.concatenate([code.astype(BF16), ones], axis=0))
        pick[:, pl.ds(member * 128, 128)] = (found == 0.0).astype(F32).astype(BF16)
    order = order_ref[...]
    for g in range(8):
        slots = (g * 16 + EP_FIRST) % 128
        part = dot(order, own_ref[pl.ds(g * 256, 256), :]).astype(BF16)
        for f in range(8):
            for member in range(2):
                first = (f * 2 + member) * 16
                rows[pl.ds(member * 128 + slots, 16), pl.ds(f * 128, 128)] = part[first : first + 16]
    for member in range(2):
        at = pl.ds(member * 128, 128)
        value = rows[at, :].astype(F32)
        inverse = lax.rsqrt(jnp.mean(value * value, axis=1, keepdims=True) + 1e-06)
        normed_ref[at, 0:1024] = (value * inverse).astype(BF16)
    for part in range(2):
        at = pl.ds(part * 384, 384)
        send_ref[at, :] = dot(pick[at, :], normed_ref[0:256, 0:1024]).astype(BF16)
    normed_ref[256:384, 0:1024] = rows[pl.ds(pl.multiple_of((zp & 1) * 128, 128), 128), :]


def gate_kernel(normed_ref, router_ref, mix_ref):
    mix_ref[256:384, :] = normed_ref[256:384, 0:1024]
    expand = expand_matrix(my_zp())
    wanted = item_code(iota((128, 768), 1))
    for member in range(2):
        at = pl.ds(member * 128, 128)
        code = normed_ref[at, 1024:1152]
        logits = dot(normed_ref[at, 0:1024], router_ref[...])
        weights = jnp.where(code.astype(F32) >= 0.0, jnp.exp(logits), 0.0)
        gates = weights / jnp.sum(weights, axis=1, keepdims=True)
        found = dot_nt(code, expand)
        spread = dot_nt(gates.astype(BF16), expand)
        mix_ref[at, 0:768] = jnp.where(found == wanted, spread, 0.0).astype(BF16)


def expert_kernel(x_ref, gate_ref, up_ref, down_ref, out_hbm, hidden, stage, sems):
    x = x_ref[...]

    def act(gate, up):
        return (gate / (1.0 + jnp.exp(-gate)) * up).astype(BF16)

    hidden[:, 0:256] = act(dot(x, gate_ref[0, :, 0:256]), dot(x, up_ref[0, :, 0:256]))
    last = jnp.concatenate([gate_ref[0, :, 256:384], up_ref[0, :, 256:384]], axis=1)
    both = dot(x, last)
    hidden[:, 256:384] = act(both[:, 0:128], both[:, 128:256])
    copies = []
    for i in range(4):
        lanes = pl.ds(i * 256, 256)
        stage[:, lanes] = dot(hidden[...], down_ref[0, :, lanes]).astype(BF16)
        copies.append(pltpu.make_async_copy(stage.at[:, lanes], out_hbm.at[:, lanes], sems.at[i]))
        copies[-1].start()
    for copy in copies:
        copy.wait()


def mix_kernel(mix_ref, back_ref, two_ref, one_ref, three_ref, own_ref, total):
    zp = my_zp()
    total[...] = dot(mix_ref[0:256, 0:768], back_ref[...])
    for k, ref in ((2, two_ref), (1, one_ref), (3, three_ref), (0, own_ref)):
        value = total[pl.ds(pl.multiple_of(((zp + k) & 1) * 128, 128), 128), :]
        if k == 0:
            value = value + mix_ref[256:384, :].astype(F32)
        ref[...] = value.astype(ref.dtype)


def sum_kernel(own_ref, two_ref, one_ref, three_ref, mine_ref, other_ref):
    for ref, lanes in zip((other_ref, mine_ref), halves()[::-1]):
        total = own_ref[:, lanes] + two_ref[:, lanes].astype(F32)
        total = total + one_ref[:, lanes].astype(F32)
        ref[...] = (total + three_ref[:, lanes].astype(F32)).astype(BF16)


def call(kernel, outs, ins, scratch=(), specs=None, out_spec=VMEM):
    return pl.pallas_call(
        kernel,
        out_shape=[jax.ShapeDtypeStruct(shape, dtype) for shape, dtype in outs],
        in_specs=specs or [VMEM] * len(ins),
        out_specs=[out_spec] * len(outs),
        scratch_shapes=list(scratch),
        compiler_params=PARAMS,
    )(*ins)


def pinned(x):
    return pltpu.with_memory_space_constraint(x, pltpu.HBM)


def further(i, k):
    return (i & ~7) + ((i + 2 * k) & 7)


def send_to(x, pairs):
    return lax.ppermute(x, ("group", "ep"), [(a * 128 + i, b * 128 + j) for (a, i), (b, j) in pairs])


def exchange(x, groups):
    return lax.all_to_all(x, "ep", 0, 0, axis_index_groups=groups, tiled=True)


def body(
    thinker_rows,
    owner_map,
    talker_ids,
    project_weight,
    router_weight,
    expert_gate,
    expert_up,
    expert_down,
):
    chips = range(128)
    give, keep = call(
        project_kernel,
        [((64, 1024), F32)] * 2,
        (pinned(thinker_rows), pinned(owner_map.reshape(1, 128)), pinned(project_weight)),
        [pltpu.VMEM((128, 1024), BF16), pltpu.VMEM((1024, 1024), BF16), pltpu.SemaphoreType.DMA],
        [VMEM, VMEM, HBM],
    )
    got = lax.ppermute(give, "group", SWAP)
    chosen, order = call(prepare_kernel, [((256, 64), BF16), ((256, 256), BF16)], ())
    (sent,) = call(spread_kernel, [((2048, 128), BF16)], (keep, got, chosen, order))
    own_ids = talker_ids.T
    ids = [own_ids]
    for k in (1, 2, 3):
        ids.append(send_to(own_ids, [((1, i), (1, further(i, k))) for i in chips]))
    ids = jnp.stack(ids)
    sent, ids = lax.optimization_barrier((sent, ids))
    own = exchange(sent.reshape(128, 16, 128), EP)
    got_ids = send_to(ids, [((1, i), (0, i)) for i in chips])
    own, got_ids = lax.optimization_barrier((own, got_ids))
    order, expand = call(setup_kernel, [((256, 256), BF16), ((768, 256), BF16)], ())
    send, normed = call(
        dispatch_kernel,
        [((768, 1024), BF16), ((384, 1152), BF16)],
        (own.reshape(2048, 128), order, expand, ids, got_ids),
        [pltpu.VMEM((256, 1024), BF16), pltpu.VMEM((768, 256), BF16)],
    )
    items = exchange(send.reshape(32, 24, 1024), REGIONS)
    (mix,) = call(gate_kernel, [((384, 1024), BF16)], (normed, router_weight))
    (expert_out,) = call(
        expert_kernel,
        [((768, 1024), BF16)],
        (items.reshape(768, 1024), expert_gate, expert_up, expert_down),
        [
            pltpu.VMEM((768, 384), BF16),
            pltpu.VMEM((768, 1024), BF16),
            pltpu.SemaphoreType.DMA((4,)),
        ],
        out_spec=HBM,
    )
    back = exchange(expert_out.reshape(32, 24, 1024), REGIONS)
    two, one, three, total = call(
        mix_kernel,
        [((128, 1024), BF16)] * 3 + [((128, 1024), F32)],
        (mix, back.reshape(768, 1024)),
        [pltpu.VMEM((256, 1024), F32)],
    )
    parts = []
    for k, part in ((2, two), (1, one), (3, three)):
        ends = [(i, further(i, k)) for i in chips]
        parts.append(send_to(part, [((j >> 2 & 1, i), (j >> 2 & 1, j)) for i, j in ends]))
    mine, other = call(sum_kernel, [((128, 512), BF16)] * 2, (total, *parts))
    swapped = send_to(other, [((i >> 2 & 1, i), (1 - (i >> 2 & 1), i)) for i in chips])
    return jnp.where(lax.axis_index("group") == my_zp() >> 1, mine, swapped)


def solution(mesh):
    return jax.shard_map(
        body,
        mesh=mesh,
        in_specs=(
            P("ep", "group"),
            P("ep", None),
            P("ep", None),
            P("group", None),
            P(),
            P("ep", None, None),
            P("ep", None, None),
            P("ep", None, None),
        ),
        out_specs=P("ep", "group"),
        check_vma=False,
    )
```

```python
import jax
import jax.numpy as jnp
from jax import lax
from jax.experimental import pallas as pl
from jax.experimental.pallas import tpu as pltpu
from jax.sharding import PartitionSpec as P

F32 = jnp.float32
BF16 = jnp.bfloat16
I32 = jnp.int32
EP_FIRST = 112
REGION_FIRST = 21
EP = [[(r + EP_FIRST) % 128 for r in range(128)]]
REGIONS = [
    [(i & 15) * 8 + zp * 2 + (i >> 4) for i in ((r + REGION_FIRST) % 32 for r in range(32))]
    for zp in range(4)
]
SWAP = [(0, 1), (1, 0)]
VMEM = pl.BlockSpec(memory_space=pltpu.VMEM)
HBM = pl.BlockSpec(memory_space=pltpu.HBM)
PARAMS = pltpu.CompilerParams(vmem_limit_bytes=16 * 1024 * 1024)


def my_zp():
    return (lax.axis_index("ep") >> 1) & 3


def iota(shape, dim):
    return lax.broadcasted_iota(I32, shape, dim)


def dot(a, b):
    return jnp.dot(a, b, preferred_element_type=F32)


def dot_nt(a, b):
    return lax.dot_general(a, b, (((1,), (1,)), ((), ())), preferred_element_type=F32)


def dot_tn(a, b):
    return lax.dot_general(a, b, (((0,), (0,)), ((), ())), preferred_element_type=F32)


def quantize(x_ref, out_ref):
    rows = x_ref.shape[0]
    r = iota((128, 128), 0)
    lane = iota((128, 128), 1)
    compact = jnp.zeros((rows, 128), F32)
    for b in range(8):
        largest = jnp.abs(x_ref[:, pl.ds(b * 128, 128)].astype(F32))
        for step in (16, 8, 4, 2, 1):
            largest = jnp.maximum(largest, pltpu.roll(largest, 128 - step, 1))
        first = (lane == r + b) & ((r & 31) == 0)
        compact = compact + dot(largest.astype(BF16), first.astype(F32).astype(BF16))
    power = jnp.full(compact.shape, 2.0**-31, F32)
    inverse = jnp.full(compact.shape, 2.0**31, F32)
    for step in (32, 16, 8, 4, 2, 1):
        larger = power * 2.0**step
        below = larger * 448.0 < compact
        power = jnp.where(below, larger, power)
        inverse = jnp.where(below, inverse * 2.0**-step, inverse)
    spacing = (jnp.minimum(power * 2.0, 16.0) * 2.0**-9).astype(BF16)
    inverse = (jnp.maximum(inverse * 0.5, 0.0625) * 2.0**9).astype(BF16)
    for b in range(8):
        lanes = pl.ds(b * 128, 128)
        spread = (r == (lane & 96) + b).astype(F32).astype(BF16)
        x = x_ref[:, lanes].astype(F32)
        size = jnp.abs(x) * 0.125
        level = dot(spacing, spread)
        over = dot(inverse, spread)
        for step in (8, 4, 2, 1):
            larger = level * 2.0**step
            reached = larger <= size
            level = jnp.where(reached, larger, level)
            over = jnp.where(reached, over * 2.0**-step, over)
        out_ref[:, lanes] = (jnp.floor(x * over + 0.5) * level).astype(BF16)


def halves():
    core = lax.axis_index("group")
    mine = pl.ds(pl.multiple_of(core * 512, 512), 512)
    other = pl.ds(pl.multiple_of((1 - core) * 512, 512), 512)
    return mine, other


def project_kernel(x_ref, owner_ref, w_hbm, give_ref, keep_ref, restored, weight, sem):
    copy = pltpu.make_async_copy(w_hbm, weight, sem)
    copy.start()
    quantize(x_ref, restored)
    core = lax.axis_index("group")
    n = iota((128, 128), 0)
    half = jnp.where(n < 64, 1 - core, core)
    owner = ((((n & 63) >> 2) * 4 + half * 2 + (n & 1)) << 1) + ((n >> 1) & 1)
    chosen = (owner_ref[...] == owner).astype(F32).astype(BF16)
    rows = dot(chosen, restored[...]).astype(BF16)
    copy.wait()
    both = dot(rows, weight[...])
    give_ref[...] = both[0:64]
    keep_ref[...] = both[64:128]


def by24(n):
    return (n * 2731) >> 16


def prepare_kernel(chosen_ref, order_ref):
    a = iota((256, 64), 0)
    e = ((a >> 1) + EP_FIRST) & 127
    chosen = iota((256, 64), 1) == (((e >> 3) << 1) + (e & 1)) * 2 + (a & 1)
    chosen_ref[...] = chosen.astype(F32).astype(BF16)
    a = iota((256, 256), 0)
    source = (((a >> 1) & 7) << 5) + ((a >> 4) << 1) + (a & 1)
    order_ref[...] = (iota((256, 256), 1) == source).astype(F32).astype(BF16)


def spread_kernel(keep_ref, got_ref, chosen_ref, order_ref, out_ref):
    projected = (keep_ref[...] + got_ref[...]).astype(BF16)
    rows = dot(chosen_ref[...], projected).astype(BF16)
    order = order_ref[...]
    for g in range(8):
        part = rows[g * 32 : (g + 1) * 32]
        stack = jnp.concatenate([part[:, f * 128 : (f + 1) * 128] for f in range(8)], axis=0)
        out_ref[pl.ds(g * 256, 256), :] = dot(order, stack).astype(BF16)


def expand_matrix(zp):
    e = (by24(iota((768, 128), 0)) + REGION_FIRST) & 31
    return (iota((768, 128), 1) == ((e & 15) << 3) + zp * 2 + (e >> 4)).astype(BF16)


def item_code(n):
    r = n - by24(n) * 24
    return jnp.where(r < 12, r, r + 4).astype(F32)


def setup_kernel(order_ref, expand_ref):
    a = iota((256, 256), 0)
    order_ref[...] = (iota((256, 256), 1) == ((a & 15) << 4) + (a >> 4)).astype(F32).astype(BF16)
    expand_ref[:, 0:128] = expand_matrix(my_zp())
    taken = item_code(iota((768, 128), 0))
    expand_ref[:, 128:256] = jnp.where(iota((768, 128), 1) == 0, -taken, 0.0).astype(BF16)


def dispatch_kernel(
    own_ref, order_ref, expand_ref, ids_ref, ids_got_ref, send_ref, normed_ref, rows, pick
):
    core = lax.axis_index("group")
    zp = my_zp()
    expert = iota((128, 128), 0)
    earlier = (expert < iota((128, 128), 1)).astype(F32).astype(BF16)
    expand = expand_ref[...]
    ones = jnp.ones((128, 128), BF16)
    for member in range(2):
        k = (zp + 4 - core * 2 - member) & 3
        ids = jnp.where(core == 1, ids_ref[k], ids_got_ref[k])
        named = expert == ids[0:1, :]
        for t in range(1, 8):
            named = named | (expert == ids[t : t + 1, :])
        rank = dot(named.astype(F32).astype(BF16), earlier)
        code = jnp.where(named, rank + 16.0 * member, -1.0)
        normed_ref[pl.ds(member * 128, 128), 1024:1152] = code.T.astype(BF16)
        found = dot(expand, jnp.concatenate([code.astype(BF16), ones], axis=0))
        pick[:, pl.ds(member * 128, 128)] = (found == 0.0).astype(F32).astype(BF16)
    order = order_ref[...]
    for g in range(8):
        slots = (g * 16 + EP_FIRST) % 128
        part = dot(order, own_ref[pl.ds(g * 256, 256), :]).astype(BF16)
        for f in range(8):
            for member in range(2):
                first = (f * 2 + member) * 16
                rows[pl.ds(member * 128 + slots, 16), pl.ds(f * 128, 128)] = part[first : first + 16]
    for member in range(2):
        at = pl.ds(member * 128, 128)
        value = rows[at, :].astype(F32)
        inverse = lax.rsqrt(jnp.mean(value * value, axis=1, keepdims=True) + 1e-06)
        normed_ref[at, 0:1024] = (value * inverse).astype(BF16)
    for part in range(2):
        at = pl.ds(part * 384, 384)
        send_ref[at, :] = dot(pick[at, :], normed_ref[0:256, 0:1024]).astype(BF16)
    normed_ref[256:384, 0:1024] = rows[pl.ds(pl.multiple_of((zp & 1) * 128, 128), 128), :]


def gate_kernel(normed_ref, router_ref, mix_ref):
    mix_ref[256:384, :] = normed_ref[256:384, 0:1024]
    expand = expand_matrix(my_zp())
    wanted = item_code(iota((128, 768), 1))
    for member in range(2):
        at = pl.ds(member * 128, 128)
        code = normed_ref[at, 1024:1152]
        logits = dot(normed_ref[at, 0:1024], router_ref[...])
        weights = jnp.where(code.astype(F32) >= 0.0, jnp.exp(logits), 0.0)
        gates = weights / jnp.sum(weights, axis=1, keepdims=True)
        found = dot_nt(code, expand)
        spread = dot_nt(gates.astype(BF16), expand)
        mix_ref[at, 0:768] = jnp.where(found == wanted, spread, 0.0).astype(BF16)


def expert_kernel(x_ref, gate_ref, up_ref, down_ref, out_hbm, hidden, stage, sems):
    x = x_ref[...]

    def act(gate, up):
        return (gate / (1.0 + jnp.exp(-gate)) * up).astype(BF16)

    hidden[:, 0:256] = act(dot(x, gate_ref[0, :, 0:256]), dot(x, up_ref[0, :, 0:256]))
    last = jnp.concatenate([gate_ref[0, :, 256:384], up_ref[0, :, 256:384]], axis=1)
    both = dot(x, last)
    hidden[:, 256:384] = act(both[:, 0:128], both[:, 128:256])
    copies = []
    for i in range(4):
        lanes = pl.ds(i * 256, 256)
        stage[:, lanes] = dot(hidden[...], down_ref[0, :, lanes]).astype(BF16)
        copies.append(pltpu.make_async_copy(stage.at[:, lanes], out_hbm.at[:, lanes], sems.at[i]))
        copies[-1].start()
    for copy in copies:
        copy.wait()


def mix_kernel(mix_ref, back_ref, two_ref, one_ref, three_ref, own_ref, total):
    zp = my_zp()
    total[...] = dot(mix_ref[0:256, 0:768], back_ref[...])
    for k, ref in ((2, two_ref), (1, one_ref), (3, three_ref), (0, own_ref)):
        value = total[pl.ds(pl.multiple_of(((zp + k) & 1) * 128, 128), 128), :]
        if k == 0:
            value = value + mix_ref[256:384, :].astype(F32)
        ref[...] = value.astype(ref.dtype)


def sum_kernel(own_ref, two_ref, one_ref, three_ref, mine_ref, other_ref):
    for ref, lanes in zip((other_ref, mine_ref), halves()[::-1]):
        total = own_ref[:, lanes] + two_ref[:, lanes].astype(F32)
        total = total + one_ref[:, lanes].astype(F32)
        ref[...] = (total + three_ref[:, lanes].astype(F32)).astype(BF16)


def call(kernel, outs, ins, scratch=(), specs=None, out_spec=VMEM):
    return pl.pallas_call(
        kernel,
        out_shape=[jax.ShapeDtypeStruct(shape, dtype) for shape, dtype in outs],
        in_specs=specs or [VMEM] * len(ins),
        out_specs=[out_spec] * len(outs),
        scratch_shapes=list(scratch),
        compiler_params=PARAMS,
    )(*ins)


def pinned(x):
    return pltpu.with_memory_space_constraint(x, pltpu.HBM)


def further(i, k):
    return (i & ~7) + ((i + 2 * k) & 7)


def send_to(x, pairs):
    return lax.ppermute(x, ("group", "ep"), [(a * 128 + i, b * 128 + j) for (a, i), (b, j) in pairs])


def exchange(x, groups):
    return lax.all_to_all(x, "ep", 0, 0, axis_index_groups=groups, tiled=True)


def body(
    thinker_rows,
    owner_map,
    talker_ids,
    project_weight,
    router_weight,
    expert_gate,
    expert_up,
    expert_down,
):
    chips = range(128)
    give, keep = call(
        project_kernel,
        [((64, 1024), F32)] * 2,
        (pinned(thinker_rows), pinned(owner_map.reshape(1, 128)), pinned(project_weight)),
        [pltpu.VMEM((128, 1024), BF16), pltpu.VMEM((1024, 1024), BF16), pltpu.SemaphoreType.DMA],
        [VMEM, VMEM, HBM],
    )
    got = lax.ppermute(give, "group", SWAP)
    chosen, order = call(prepare_kernel, [((256, 64), BF16), ((256, 256), BF16)], ())
    (sent,) = call(spread_kernel, [((2048, 128), BF16)], (keep, got, chosen, order))
    own_ids = talker_ids.T
    ids = [own_ids]
    for k in (1, 2, 3):
        ids.append(send_to(own_ids, [((1, i), (1, further(i, k))) for i in chips]))
    ids = jnp.stack(ids)
    sent, ids = lax.optimization_barrier((sent, ids))
    own = exchange(sent.reshape(128, 16, 128), EP)
    copies = lax.optimization_barrier(jnp.broadcast_to(ids[None], (64, 4, 8, 128)))
    got_ids = send_to(copies, [((1, i), (0, i)) for i in chips])
    own, got_ids = lax.optimization_barrier((own, got_ids))
    order, expand = call(setup_kernel, [((256, 256), BF16), ((768, 256), BF16)], ())
    send, normed = call(
        dispatch_kernel,
        [((768, 1024), BF16), ((384, 1152), BF16)],
        (own.reshape(2048, 128), order, expand, ids, got_ids[0]),
        [pltpu.VMEM((256, 1024), BF16), pltpu.VMEM((768, 256), BF16)],
    )
    items = exchange(send.reshape(32, 24, 1024), REGIONS)
    (mix,) = call(gate_kernel, [((384, 1024), BF16)], (normed, router_weight))
    (expert_out,) = call(
        expert_kernel,
        [((768, 1024), BF16)],
        (items.reshape(768, 1024), expert_gate, expert_up, expert_down),
        [
            pltpu.VMEM((768, 384), BF16),
            pltpu.VMEM((768, 1024), BF16),
            pltpu.SemaphoreType.DMA((4,)),
        ],
        out_spec=HBM,
    )
    back = exchange(expert_out.reshape(32, 24, 1024), REGIONS)
    two, one, three, total = call(
        mix_kernel,
        [((128, 1024), BF16)] * 3 + [((128, 1024), F32)],
        (mix, back.reshape(768, 1024)),
        [pltpu.VMEM((256, 1024), F32)],
    )
    parts = []
    for k, part in ((2, two), (1, one), (3, three)):
        ends = [(i, further(i, k)) for i in chips]
        parts.append(send_to(part, [((j >> 2 & 1, i), (j >> 2 & 1, j)) for i, j in ends]))
    mine, other = call(sum_kernel, [((128, 512), BF16)] * 2, (total, *parts))
    swapped = send_to(other, [((i >> 2 & 1, i), (1 - (i >> 2 & 1), i)) for i in chips])
    return jnp.where(lax.axis_index("group") == my_zp() >> 1, mine, swapped)


def solution(mesh):
    return jax.shard_map(
        body,
        mesh=mesh,
        in_specs=(
            P("ep", "group"),
            P("ep", None),
            P("ep", None),
            P("group", None),
            P(),
            P("ep", None, None),
            P("ep", None, None),
            P("ep", None, None),
        ),
        out_specs=P("ep", "group"),
        check_vma=False,
    )
```

```python
import jax
import jax.numpy as jnp
from jax import lax
from jax.experimental import pallas as pl
from jax.experimental.pallas import tpu as pltpu
from jax.sharding import PartitionSpec as P

F32 = jnp.float32
BF16 = jnp.bfloat16
I32 = jnp.int32
EP_FIRST = 112
REGION_FIRST = 21
EP = [[(r + EP_FIRST) % 128 for r in range(128)]]
REGIONS = [
    [(i & 15) * 8 + zp * 2 + (i >> 4) for i in ((r + REGION_FIRST) % 32 for r in range(32))]
    for zp in range(4)
]
SWAP = [(0, 1), (1, 0)]
VMEM = pl.BlockSpec(memory_space=pltpu.VMEM)
HBM = pl.BlockSpec(memory_space=pltpu.HBM)
PARAMS = pltpu.CompilerParams(vmem_limit_bytes=16 * 1024 * 1024)


def my_zp():
    return (lax.axis_index("ep") >> 1) & 3


def iota(shape, dim):
    return lax.broadcasted_iota(I32, shape, dim)


def dot(a, b):
    return jnp.dot(a, b, preferred_element_type=F32)


def dot_nt(a, b):
    return lax.dot_general(a, b, (((1,), (1,)), ((), ())), preferred_element_type=F32)


def dot_tn(a, b):
    return lax.dot_general(a, b, (((0,), (0,)), ((), ())), preferred_element_type=F32)


def quantize(x_ref, out_ref):
    rows = x_ref.shape[0]
    r = iota((128, 128), 0)
    lane = iota((128, 128), 1)
    compact = jnp.zeros((rows, 128), F32)
    for b in range(8):
        largest = jnp.abs(x_ref[:, pl.ds(b * 128, 128)].astype(F32))
        for step in (16, 8, 4, 2, 1):
            largest = jnp.maximum(largest, pltpu.roll(largest, 128 - step, 1))
        first = (lane == r + b) & ((r & 31) == 0)
        compact = compact + dot(largest.astype(BF16), first.astype(F32).astype(BF16))
    power = jnp.full(compact.shape, 2.0**-31, F32)
    inverse = jnp.full(compact.shape, 2.0**31, F32)
    for step in (32, 16, 8, 4, 2, 1):
        larger = power * 2.0**step
        below = larger * 448.0 < compact
        power = jnp.where(below, larger, power)
        inverse = jnp.where(below, inverse * 2.0**-step, inverse)
    spacing = (jnp.minimum(power * 2.0, 16.0) * 2.0**-9).astype(BF16)
    inverse = (jnp.maximum(inverse * 0.5, 0.0625) * 2.0**9).astype(BF16)
    for b in range(8):
        lanes = pl.ds(b * 128, 128)
        spread = (r == (lane & 96) + b).astype(F32).astype(BF16)
        x = x_ref[:, lanes].astype(F32)
        size = jnp.abs(x) * 0.125
        level = dot(spacing, spread)
        over = dot(inverse, spread)
        for step in (8, 4, 2, 1):
            larger = level * 2.0**step
            reached = larger <= size
            level = jnp.where(reached, larger, level)
            over = jnp.where(reached, over * 2.0**-step, over)
        out_ref[:, lanes] = (jnp.floor(x * over + 0.5) * level).astype(BF16)


def halves():
    core = lax.axis_index("group")
    mine = pl.ds(pl.multiple_of(core * 512, 512), 512)
    other = pl.ds(pl.multiple_of((1 - core) * 512, 512), 512)
    return mine, other


def project_kernel(x_ref, owner_ref, w_hbm, give_ref, keep_ref, restored, weight, sem):
    copy = pltpu.make_async_copy(w_hbm, weight, sem)
    copy.start()
    quantize(x_ref, restored)
    core = lax.axis_index("group")
    n = iota((128, 128), 0)
    half = jnp.where(n < 64, 1 - core, core)
    owner = ((((n & 63) >> 2) * 4 + half + (n & 1) * 2) << 1) + ((n >> 1) & 1)
    chosen = (owner_ref[...] == owner).astype(F32).astype(BF16)
    rows = dot(chosen, restored[...]).astype(BF16)
    copy.wait()
    both = dot(rows, weight[...])
    give_ref[...] = both[0:64]
    keep_ref[...] = both[64:128]


def by24(n):
    return (n * 2731) >> 16


def prepare_kernel(chosen_ref, order_ref):
    a = iota((256, 64), 0)
    e = ((a >> 1) + EP_FIRST) & 127
    chosen = iota((256, 64), 1) == (((e >> 3) << 1) + (e & 1)) * 2 + (a & 1)
    chosen_ref[...] = chosen.astype(F32).astype(BF16)
    a = iota((256, 256), 0)
    source = (((a >> 1) & 7) << 5) + ((a >> 4) << 1) + (a & 1)
    order_ref[...] = (iota((256, 256), 1) == source).astype(F32).astype(BF16)


def spread_kernel(keep_ref, got_ref, chosen_ref, order_ref, out_ref):
    projected = (keep_ref[...] + got_ref[...]).astype(BF16)
    rows = dot(chosen_ref[...], projected).astype(BF16)
    order = order_ref[...]
    for g in range(8):
        part = rows[g * 32 : (g + 1) * 32]
        stack = jnp.concatenate([part[:, f * 128 : (f + 1) * 128] for f in range(8)], axis=0)
        out_ref[pl.ds(g * 256, 256), :] = dot(order, stack).astype(BF16)


def expand_matrix(zp):
    e = (by24(iota((768, 128), 0)) + REGION_FIRST) & 31
    return (iota((768, 128), 1) == ((e & 15) << 3) + zp * 2 + (e >> 4)).astype(BF16)


def item_code(n):
    r = n - by24(n) * 24
    return jnp.where(r < 12, r, r + 4).astype(F32)


def setup_kernel(order_ref, expand_ref):
    a = iota((256, 256), 0)
    order_ref[...] = (iota((256, 256), 1) == ((a & 15) << 4) + (a >> 4)).astype(F32).astype(BF16)
    expand_ref[:, 0:128] = expand_matrix(my_zp())
    taken = item_code(iota((768, 128), 0))
    expand_ref[:, 128:256] = jnp.where(iota((768, 128), 1) == 0, -taken, 0.0).astype(BF16)


def dispatch_kernel(
    own_ref, order_ref, expand_ref, ids_ref, ids_got_ref, send_ref, normed_ref, rows, pick
):
    core = lax.axis_index("group")
    zp = my_zp()
    expert = iota((128, 128), 0)
    earlier = (expert < iota((128, 128), 1)).astype(F32).astype(BF16)
    expand = expand_ref[...]
    ones = jnp.ones((128, 128), BF16)
    for member in range(2):
        k = (zp + 4 - core - 2 * member) & 3
        ids = jnp.where(core == 1, ids_ref[k], ids_got_ref[k])
        named = expert == ids[0:1, :]
        for t in range(1, 8):
            named = named | (expert == ids[t : t + 1, :])
        rank = dot(named.astype(F32).astype(BF16), earlier)
        code = jnp.where(named, rank + 16.0 * member, -1.0)
        normed_ref[pl.ds(member * 128, 128), 1024:1152] = code.T.astype(BF16)
        found = dot(expand, jnp.concatenate([code.astype(BF16), ones], axis=0))
        pick[:, pl.ds(member * 128, 128)] = (found == 0.0).astype(F32).astype(BF16)
    order = order_ref[...]
    for g in range(8):
        slots = (g * 16 + EP_FIRST) % 128
        part = dot(order, own_ref[pl.ds(g * 256, 256), :]).astype(BF16)
        for f in range(8):
            for member in range(2):
                first = (f * 2 + member) * 16
                rows[pl.ds(member * 128 + slots, 16), pl.ds(f * 128, 128)] = part[first : first + 16]
    for member in range(2):
        at = pl.ds(member * 128, 128)
        value = rows[at, :].astype(F32)
        inverse = lax.rsqrt(jnp.mean(value * value, axis=1, keepdims=True) + 1e-06)
        normed_ref[at, 0:1024] = (value * inverse).astype(BF16)
    for part in range(2):
        at = pl.ds(part * 384, 384)
        send_ref[at, :] = dot(pick[at, :], normed_ref[0:256, 0:1024]).astype(BF16)
    normed_ref[256:384, 0:1024] = rows[pl.ds(pl.multiple_of((zp >> 1) * 128, 128), 128), :]


def gate_kernel(normed_ref, router_ref, mix_ref):
    mix_ref[256:384, :] = normed_ref[256:384, 0:1024]
    expand = expand_matrix(my_zp())
    wanted = item_code(iota((128, 768), 1))
    for member in range(2):
        at = pl.ds(member * 128, 128)
        code = normed_ref[at, 1024:1152]
        logits = dot(normed_ref[at, 0:1024], router_ref[...])
        weights = jnp.where(code.astype(F32) >= 0.0, jnp.exp(logits), 0.0)
        gates = weights / jnp.sum(weights, axis=1, keepdims=True)
        found = dot_nt(code, expand)
        spread = dot_nt(gates.astype(BF16), expand)
        mix_ref[at, 0:768] = jnp.where(found == wanted, spread, 0.0).astype(BF16)


def expert_kernel(x_ref, gate_ref, up_ref, down_ref, out_hbm, hidden, stage, sems):
    x = x_ref[...]

    def act(gate, up):
        return (gate / (1.0 + jnp.exp(-gate)) * up).astype(BF16)

    hidden[:, 0:256] = act(dot(x, gate_ref[0, :, 0:256]), dot(x, up_ref[0, :, 0:256]))
    last = jnp.concatenate([gate_ref[0, :, 256:384], up_ref[0, :, 256:384]], axis=1)
    both = dot(x, last)
    hidden[:, 256:384] = act(both[:, 0:128], both[:, 128:256])
    copies = []
    for i in range(4):
        lanes = pl.ds(i * 256, 256)
        stage[:, lanes] = dot(hidden[...], down_ref[0, :, lanes]).astype(BF16)
        copies.append(pltpu.make_async_copy(stage.at[:, lanes], out_hbm.at[:, lanes], sems.at[i]))
        copies[-1].start()
    for copy in copies:
        copy.wait()


def mix_kernel(mix_ref, back_ref, two_ref, one_ref, three_ref, own_ref, total):
    zp = my_zp()
    total[...] = dot(mix_ref[0:256, 0:768], back_ref[...])
    for k, ref in ((2, two_ref), (1, one_ref), (3, three_ref), (0, own_ref)):
        value = total[pl.ds(pl.multiple_of((((zp + k) & 3) >> 1) * 128, 128), 128), :]
        if k == 0:
            value = value + mix_ref[256:384, :].astype(F32)
        ref[...] = value.astype(ref.dtype)


def sum_kernel(own_ref, two_ref, one_ref, three_ref, mine_ref, other_ref):
    for ref, lanes in zip((other_ref, mine_ref), halves()[::-1]):
        total = own_ref[:, lanes] + two_ref[:, lanes].astype(F32)
        total = total + one_ref[:, lanes].astype(F32)
        ref[...] = (total + three_ref[:, lanes].astype(F32)).astype(BF16)


def call(kernel, outs, ins, scratch=(), specs=None, out_spec=VMEM):
    return pl.pallas_call(
        kernel,
        out_shape=[jax.ShapeDtypeStruct(shape, dtype) for shape, dtype in outs],
        in_specs=specs or [VMEM] * len(ins),
        out_specs=[out_spec] * len(outs),
        scratch_shapes=list(scratch),
        compiler_params=PARAMS,
    )(*ins)


def pinned(x):
    return pltpu.with_memory_space_constraint(x, pltpu.HBM)


def further(i, k):
    return (i & ~7) + ((i + 2 * k) & 7)


def send_to(x, pairs):
    return lax.ppermute(x, ("group", "ep"), [(a * 128 + i, b * 128 + j) for (a, i), (b, j) in pairs])


def exchange(x, groups):
    return lax.all_to_all(x, "ep", 0, 0, axis_index_groups=groups, tiled=True)


def body(
    thinker_rows,
    owner_map,
    talker_ids,
    project_weight,
    router_weight,
    expert_gate,
    expert_up,
    expert_down,
):
    chips = range(128)
    give, keep = call(
        project_kernel,
        [((64, 1024), F32)] * 2,
        (pinned(thinker_rows), pinned(owner_map.reshape(1, 128)), pinned(project_weight)),
        [pltpu.VMEM((128, 1024), BF16), pltpu.VMEM((1024, 1024), BF16), pltpu.SemaphoreType.DMA],
        [VMEM, VMEM, HBM],
    )
    got = lax.ppermute(give, "group", SWAP)
    chosen, order = call(prepare_kernel, [((256, 64), BF16), ((256, 256), BF16)], ())
    (sent,) = call(spread_kernel, [((2048, 128), BF16)], (keep, got, chosen, order))
    own_ids = talker_ids.T
    ids = [own_ids]
    for k in (1, 2, 3):
        ids.append(send_to(own_ids, [((1, i), (1, further(i, k))) for i in chips]))
    ids = jnp.stack(ids)
    sent, ids = lax.optimization_barrier((sent, ids))
    own = exchange(sent.reshape(128, 16, 128), EP)
    copies = lax.optimization_barrier(jnp.broadcast_to(ids[None], (64, 4, 8, 128)))
    got_ids = send_to(copies, [((1, i), (0, i)) for i in chips])
    own, got_ids = lax.optimization_barrier((own, got_ids))
    order, expand = call(setup_kernel, [((256, 256), BF16), ((768, 256), BF16)], ())
    send, normed = call(
        dispatch_kernel,
        [((768, 1024), BF16), ((384, 1152), BF16)],
        (own.reshape(2048, 128), order, expand, ids, got_ids[0]),
        [pltpu.VMEM((256, 1024), BF16), pltpu.VMEM((768, 256), BF16)],
    )
    items = exchange(send.reshape(32, 24, 1024), REGIONS)
    (mix,) = call(gate_kernel, [((384, 1024), BF16)], (normed, router_weight))
    (expert_out,) = call(
        expert_kernel,
        [((768, 1024), BF16)],
        (items.reshape(768, 1024), expert_gate, expert_up, expert_down),
        [
            pltpu.VMEM((768, 384), BF16),
            pltpu.VMEM((768, 1024), BF16),
            pltpu.SemaphoreType.DMA((4,)),
        ],
        out_spec=HBM,
    )
    back = exchange(expert_out.reshape(32, 24, 1024), REGIONS)
    two, one, three, total = call(
        mix_kernel,
        [((128, 1024), BF16)] * 3 + [((128, 1024), F32)],
        (mix, back.reshape(768, 1024)),
        [pltpu.VMEM((256, 1024), F32)],
    )
    parts = []
    for k, part in ((1, one), (3, three), (2, two)):
        ends = [(i, further(i, k)) for i in chips]
        parts.append(send_to(part, [((j >> 1 & 1, i), (j >> 1 & 1, j)) for i, j in ends]))
    mine, other = call(sum_kernel, [((128, 512), BF16)] * 2, (total, *parts))
    swapped = send_to(other, [((i >> 1 & 1, i), (1 - (i >> 1 & 1), i)) for i in chips])
    return jnp.where(lax.axis_index("group") == my_zp() & 1, mine, swapped)


def solution(mesh):
    return jax.shard_map(
        body,
        mesh=mesh,
        in_specs=(
            P("ep", "group"),
            P("ep", None),
            P("ep", None),
            P("group", None),
            P(),
            P("ep", None, None),
            P("ep", None, None),
            P("ep", None, None),
        ),
        out_specs=P("ep", "group"),
        check_vma=False,
    )
```

```python
import jax
import jax.numpy as jnp
from jax import lax
from jax.experimental import pallas as pl
from jax.experimental.pallas import tpu as pltpu
from jax.sharding import PartitionSpec as P

F32 = jnp.float32
BF16 = jnp.bfloat16
I32 = jnp.int32
EP_FIRST = 112
REGION_FIRST = 21
EP = [[(r + EP_FIRST) % 128 for r in range(128)]]
REGIONS = [
    [(i & 15) * 8 + zp * 2 + (i >> 4) for i in ((r + REGION_FIRST) % 32 for r in range(32))]
    for zp in range(4)
]
SWAP = [(0, 1), (1, 0)]
VMEM = pl.BlockSpec(memory_space=pltpu.VMEM)
HBM = pl.BlockSpec(memory_space=pltpu.HBM)
PARAMS = pltpu.CompilerParams(vmem_limit_bytes=16 * 1024 * 1024)


def my_zp():
    return (lax.axis_index("ep") >> 1) & 3


def iota(shape, dim):
    return lax.broadcasted_iota(I32, shape, dim)


def dot(a, b):
    return jnp.dot(a, b, preferred_element_type=F32)


def dot_nt(a, b):
    return lax.dot_general(a, b, (((1,), (1,)), ((), ())), preferred_element_type=F32)


def dot_tn(a, b):
    return lax.dot_general(a, b, (((0,), (0,)), ((), ())), preferred_element_type=F32)


def quantize(x_ref, out_ref):
    rows = x_ref.shape[0]
    r = iota((128, 128), 0)
    lane = iota((128, 128), 1)
    compact = jnp.zeros((rows, 128), F32)
    for b in range(8):
        largest = jnp.abs(x_ref[:, pl.ds(b * 128, 128)].astype(F32))
        for step in (16, 8, 4, 2, 1):
            largest = jnp.maximum(largest, pltpu.roll(largest, 128 - step, 1))
        first = (lane == r + b) & ((r & 31) == 0)
        compact = compact + dot(largest.astype(BF16), first.astype(F32).astype(BF16))
    power = jnp.full(compact.shape, 2.0**-31, F32)
    inverse = jnp.full(compact.shape, 2.0**31, F32)
    for step in (32, 16, 8, 4, 2, 1):
        larger = power * 2.0**step
        below = larger * 448.0 < compact
        power = jnp.where(below, larger, power)
        inverse = jnp.where(below, inverse * 2.0**-step, inverse)
    spacing = (jnp.minimum(power * 2.0, 16.0) * 2.0**-9).astype(BF16)
    inverse = (jnp.maximum(inverse * 0.5, 0.0625) * 2.0**9).astype(BF16)
    for b in range(8):
        lanes = pl.ds(b * 128, 128)
        spread = (r == (lane & 96) + b).astype(F32).astype(BF16)
        x = x_ref[:, lanes].astype(F32)
        size = jnp.abs(x) * 0.125
        level = dot(spacing, spread)
        over = dot(inverse, spread)
        for step in (8, 4, 2, 1):
            larger = level * 2.0**step
            reached = larger <= size
            level = jnp.where(reached, larger, level)
            over = jnp.where(reached, over * 2.0**-step, over)
        out_ref[:, lanes] = (jnp.floor(x * over + 0.5) * level).astype(BF16)


def halves():
    core = lax.axis_index("group")
    mine = pl.ds(pl.multiple_of(core * 512, 512), 512)
    other = pl.ds(pl.multiple_of((1 - core) * 512, 512), 512)
    return mine, other


def project_kernel(x_ref, owner_ref, w_hbm, give_ref, keep_ref, restored, weight, sem):
    copy = pltpu.make_async_copy(w_hbm, weight, sem)
    copy.start()
    quantize(x_ref, restored)
    core = lax.axis_index("group")
    n = iota((128, 128), 0)
    half = jnp.where(n < 64, 1 - core, core)
    owner = ((((n & 63) >> 2) * 4 + half + (n & 1) * 2) << 1) + ((n >> 1) & 1)
    chosen = (owner_ref[...] == owner).astype(F32).astype(BF16)
    rows = dot(chosen, restored[...]).astype(BF16)
    copy.wait()
    both = dot(rows, weight[...])
    give_ref[...] = both[0:64]
    keep_ref[...] = both[64:128]


def by24(n):
    return (n * 2731) >> 16


def prepare_kernel(chosen_ref, order_ref):
    a = iota((256, 64), 0)
    e = ((a >> 1) + EP_FIRST) & 127
    chosen = iota((256, 64), 1) == (((e >> 3) << 1) + (e & 1)) * 2 + (a & 1)
    chosen_ref[...] = chosen.astype(F32).astype(BF16)
    a = iota((256, 256), 0)
    source = (((a >> 1) & 7) << 5) + ((a >> 4) << 1) + (a & 1)
    order_ref[...] = (iota((256, 256), 1) == source).astype(F32).astype(BF16)


def spread_kernel(keep_ref, got_ref, chosen_ref, order_ref, out_ref):
    projected = (keep_ref[...] + got_ref[...]).astype(BF16)
    rows = dot(chosen_ref[...], projected).astype(BF16)
    order = order_ref[...]
    for g in range(8):
        part = rows[g * 32 : (g + 1) * 32]
        stack = jnp.concatenate([part[:, f * 128 : (f + 1) * 128] for f in range(8)], axis=0)
        out_ref[pl.ds(g * 256, 256), :] = dot(order, stack).astype(BF16)


def expand_matrix(zp):
    e = (by24(iota((768, 128), 0)) + REGION_FIRST) & 31
    return (iota((768, 128), 1) == ((e & 15) << 3) + zp * 2 + (e >> 4)).astype(BF16)


def item_code(n):
    r = n - by24(n) * 24
    return jnp.where(r < 12, r, r + 4).astype(F32)


def setup_kernel(order_ref, expand_ref):
    a = iota((256, 256), 0)
    order_ref[...] = (iota((256, 256), 1) == ((a & 15) << 4) + (a >> 4)).astype(F32).astype(BF16)
    expand_ref[:, 0:128] = expand_matrix(my_zp())
    taken = item_code(iota((768, 128), 0))
    expand_ref[:, 128:256] = jnp.where(iota((768, 128), 1) == 0, -taken, 0.0).astype(BF16)


def dispatch_kernel(
    own_ref, order_ref, expand_ref, ids_ref, ids_got_ref, send_ref, normed_ref, rows, pick
):
    core = lax.axis_index("group")
    zp = my_zp()
    expert = iota((128, 128), 0)
    earlier = (expert < iota((128, 128), 1)).astype(F32).astype(BF16)
    expand = expand_ref[...]
    ones = jnp.ones((128, 128), BF16)
    for member in range(2):
        k = (zp + 4 - core - 2 * member) & 3
        ids = jnp.where(core == 1, ids_ref[k], ids_got_ref[k])
        named = expert == ids[0:1, :]
        for t in range(1, 8):
            named = named | (expert == ids[t : t + 1, :])
        rank = dot(named.astype(F32).astype(BF16), earlier)
        code = jnp.where(named, rank + 16.0 * member, -1.0)
        normed_ref[pl.ds(member * 128, 128), 1024:1152] = code.T.astype(BF16)
        found = dot(expand, jnp.concatenate([code.astype(BF16), ones], axis=0))
        pick[:, pl.ds(member * 128, 128)] = (found == 0.0).astype(F32).astype(BF16)
    order = order_ref[...]
    for g in range(8):
        slots = (g * 16 + EP_FIRST) % 128
        part = dot(order, own_ref[pl.ds(g * 256, 256), :]).astype(BF16)
        for f in range(8):
            for member in range(2):
                first = (f * 2 + member) * 16
                rows[pl.ds(member * 128 + slots, 16), pl.ds(f * 128, 128)] = part[first : first + 16]
    for member in range(2):
        at = pl.ds(member * 128, 128)
        value = rows[at, :].astype(F32)
        inverse = lax.rsqrt(jnp.mean(value * value, axis=1, keepdims=True) + 1e-06)
        normed_ref[at, 0:1024] = (value * inverse).astype(BF16)
    for part in range(2):
        at = pl.ds(part * 384, 384)
        send_ref[at, :] = dot(pick[at, :], normed_ref[0:256, 0:1024]).astype(BF16)
    normed_ref[256:384, 0:1024] = rows[pl.ds(pl.multiple_of((zp >> 1) * 128, 128), 128), :]


def gate_kernel(normed_ref, router_ref, mix_ref):
    mix_ref[256:384, :] = normed_ref[256:384, 0:1024]
    expand = expand_matrix(my_zp())
    wanted = item_code(iota((128, 768), 1))
    for member in range(2):
        at = pl.ds(member * 128, 128)
        code = normed_ref[at, 1024:1152]
        logits = dot(normed_ref[at, 0:1024], router_ref[...])
        weights = jnp.where(code.astype(F32) >= 0.0, jnp.exp(logits), 0.0)
        gates = weights / jnp.sum(weights, axis=1, keepdims=True)
        found = dot_nt(code, expand)
        spread = dot_nt(gates.astype(BF16), expand)
        mix_ref[at, 0:768] = jnp.where(found == wanted, spread, 0.0).astype(BF16)


def expert_kernel(x_ref, gate_ref, up_ref, down_ref, out_hbm, hidden, stage, sems):
    def act(gate, up):
        return (gate / (1.0 + jnp.exp(-gate)) * up).astype(BF16)

    last = jnp.concatenate([gate_ref[0, :, 256:384], up_ref[0, :, 256:384]], axis=1)
    copies = []
    for i in range(2):
        at = pl.ds(i * 384, 384)
        x = x_ref[at, :]
        hidden[at, 0:256] = act(dot(x, gate_ref[0, :, 0:256]), dot(x, up_ref[0, :, 0:256]))
        both = dot(x, last)
        hidden[at, 256:384] = act(both[:, 0:128], both[:, 128:256])
        stage[at, :] = dot(hidden[at, :], down_ref[0]).astype(BF16)
        for j in range(2):
            rows = pl.ds(i * 384 + j * 192, 192)
            copies.append(
                pltpu.make_async_copy(
                    stage.at[rows, :], out_hbm.at[rows, :], sems.at[i * 2 + j]
                )
            )
            copies[-1].start()
    for copy in copies:
        copy.wait()


def mix_kernel(mix_ref, back_ref, two_ref, one_ref, three_ref, own_ref, total):
    zp = my_zp()
    total[...] = dot(mix_ref[0:256, 0:768], back_ref[...])
    for k, ref in ((2, two_ref), (1, one_ref), (3, three_ref), (0, own_ref)):
        value = total[pl.ds(pl.multiple_of((((zp + k) & 3) >> 1) * 128, 128), 128), :]
        if k == 0:
            value = value + mix_ref[256:384, :].astype(F32)
        ref[...] = value.astype(ref.dtype)


def sum_kernel(own_ref, two_ref, one_ref, three_ref, mine_ref, other_ref):
    for ref, lanes in zip((other_ref, mine_ref), halves()[::-1]):
        total = own_ref[:, lanes] + two_ref[:, lanes].astype(F32)
        total = total + one_ref[:, lanes].astype(F32)
        ref[...] = (total + three_ref[:, lanes].astype(F32)).astype(BF16)


def call(kernel, outs, ins, scratch=(), specs=None, out_spec=VMEM):
    return pl.pallas_call(
        kernel,
        out_shape=[jax.ShapeDtypeStruct(shape, dtype) for shape, dtype in outs],
        in_specs=specs or [VMEM] * len(ins),
        out_specs=[out_spec] * len(outs),
        scratch_shapes=list(scratch),
        compiler_params=PARAMS,
    )(*ins)


def pinned(x):
    return pltpu.with_memory_space_constraint(x, pltpu.HBM)


def further(i, k):
    return (i & ~7) + ((i + 2 * k) & 7)


def send_to(x, pairs):
    return lax.ppermute(x, ("group", "ep"), [(a * 128 + i, b * 128 + j) for (a, i), (b, j) in pairs])


def exchange(x, groups):
    return lax.all_to_all(x, "ep", 0, 0, axis_index_groups=groups, tiled=True)


def body(
    thinker_rows,
    owner_map,
    talker_ids,
    project_weight,
    router_weight,
    expert_gate,
    expert_up,
    expert_down,
):
    chips = range(128)
    give, keep = call(
        project_kernel,
        [((64, 1024), F32)] * 2,
        (pinned(thinker_rows), pinned(owner_map.reshape(1, 128)), pinned(project_weight)),
        [pltpu.VMEM((128, 1024), BF16), pltpu.VMEM((1024, 1024), BF16), pltpu.SemaphoreType.DMA],
        [VMEM, VMEM, HBM],
    )
    got = lax.ppermute(give, "group", SWAP)
    chosen, order = call(prepare_kernel, [((256, 64), BF16), ((256, 256), BF16)], ())
    (sent,) = call(spread_kernel, [((2048, 128), BF16)], (keep, got, chosen, order))
    own_ids = talker_ids.T
    ids = [own_ids]
    for k in (1, 2, 3):
        ids.append(send_to(own_ids, [((1, i), (1, further(i, k))) for i in chips]))
    ids = jnp.stack(ids)
    sent, ids = lax.optimization_barrier((sent, ids))
    own = exchange(sent.reshape(128, 16, 128), EP)
    copies = lax.optimization_barrier(jnp.broadcast_to(ids[None], (64, 4, 8, 128)))
    got_ids = send_to(copies, [((1, i), (0, i)) for i in chips])
    own, got_ids = lax.optimization_barrier((own, got_ids))
    order, expand = call(setup_kernel, [((256, 256), BF16), ((768, 256), BF16)], ())
    send, normed = call(
        dispatch_kernel,
        [((768, 1024), BF16), ((384, 1152), BF16)],
        (own.reshape(2048, 128), order, expand, ids, got_ids[0]),
        [pltpu.VMEM((256, 1024), BF16), pltpu.VMEM((768, 256), BF16)],
    )
    items = exchange(send.reshape(32, 24, 1024), REGIONS)
    (mix,) = call(gate_kernel, [((384, 1024), BF16)], (normed, router_weight))
    (expert_out,) = call(
        expert_kernel,
        [((768, 1024), BF16)],
        (items.reshape(768, 1024), expert_gate, expert_up, expert_down),
        [
            pltpu.VMEM((768, 384), BF16),
            pltpu.VMEM((768, 1024), BF16),
            pltpu.SemaphoreType.DMA((4,)),
        ],
        out_spec=HBM,
    )
    back = exchange(expert_out.reshape(32, 24, 1024), REGIONS)
    two, one, three, total = call(
        mix_kernel,
        [((128, 1024), BF16)] * 3 + [((128, 1024), F32)],
        (mix, back.reshape(768, 1024)),
        [pltpu.VMEM((256, 1024), F32)],
    )
    parts = []
    for k, part in ((1, one), (3, three), (2, two)):
        ends = [(i, further(i, k)) for i in chips]
        parts.append(send_to(part, [((j >> 1 & 1, i), (j >> 1 & 1, j)) for i, j in ends]))
    mine, other = call(sum_kernel, [((128, 512), BF16)] * 2, (total, *parts))
    swapped = send_to(other, [((i >> 1 & 1, i), (1 - (i >> 1 & 1), i)) for i in chips])
    return jnp.where(lax.axis_index("group") == my_zp() & 1, mine, swapped)


def solution(mesh):
    return jax.shard_map(
        body,
        mesh=mesh,
        in_specs=(
            P("ep", "group"),
            P("ep", None),
            P("ep", None),
            P("group", None),
            P(),
            P("ep", None, None),
            P("ep", None, None),
            P("ep", None, None),
        ),
        out_specs=P("ep", "group"),
        check_vma=False,
    )
```

```python
import functools

import jax
import jax.numpy as jnp
from jax import lax
from jax.experimental import pallas as pl
from jax.experimental.pallas import tpu as pltpu
from jax.sharding import PartitionSpec as P

F32 = jnp.float32
BF16 = jnp.bfloat16
I32 = jnp.int32
EP_FIRST = 112
REGION_FIRST = 21
EP = [[(r + EP_FIRST) % 128 for r in range(128)]]
REGIONS = [
    [(i & 15) * 8 + zp * 2 + (i >> 4) for i in ((r + REGION_FIRST) % 32 for r in range(32))]
    for zp in range(4)
]
SWAP = [(0, 1), (1, 0)]
VMEM = pl.BlockSpec(memory_space=pltpu.VMEM)
HBM = pl.BlockSpec(memory_space=pltpu.HBM)
PARAMS = pltpu.CompilerParams(vmem_limit_bytes=16 * 1024 * 1024)


def my_zp():
    return (lax.axis_index("ep") >> 1) & 3


def iota(shape, dim):
    return lax.broadcasted_iota(I32, shape, dim)


def dot(a, b):
    return jnp.dot(a, b, preferred_element_type=F32)


def dot_nt(a, b):
    return lax.dot_general(a, b, (((1,), (1,)), ((), ())), preferred_element_type=F32)


def dot_tn(a, b):
    return lax.dot_general(a, b, (((0,), (0,)), ((), ())), preferred_element_type=F32)


def quantize(x_ref, out_ref):
    rows = x_ref.shape[0]
    r = iota((128, 128), 0)
    lane = iota((128, 128), 1)
    compact = jnp.zeros((rows, 128), F32)
    for b in range(8):
        largest = jnp.abs(x_ref[:, pl.ds(b * 128, 128)].astype(F32))
        for step in (16, 8, 4, 2, 1):
            largest = jnp.maximum(largest, pltpu.roll(largest, 128 - step, 1))
        first = (lane == r + b) & ((r & 31) == 0)
        compact = compact + dot(largest.astype(BF16), first.astype(F32).astype(BF16))
    power = jnp.full(compact.shape, 2.0**-31, F32)
    inverse = jnp.full(compact.shape, 2.0**31, F32)
    for step in (32, 16, 8, 4, 2, 1):
        larger = power * 2.0**step
        below = larger * 448.0 < compact
        power = jnp.where(below, larger, power)
        inverse = jnp.where(below, inverse * 2.0**-step, inverse)
    spacing = (jnp.minimum(power * 2.0, 16.0) * 2.0**-9).astype(BF16)
    inverse = (jnp.maximum(inverse * 0.5, 0.0625) * 2.0**9).astype(BF16)
    for b in range(8):
        lanes = pl.ds(b * 128, 128)
        spread = (r == (lane & 96) + b).astype(F32).astype(BF16)
        x = x_ref[:, lanes].astype(F32)
        size = jnp.abs(x) * 0.125
        level = dot(spacing, spread)
        over = dot(inverse, spread)
        for step in (8, 4, 2, 1):
            larger = level * 2.0**step
            reached = larger <= size
            level = jnp.where(reached, larger, level)
            over = jnp.where(reached, over * 2.0**-step, over)
        out_ref[:, lanes] = (jnp.floor(x * over + 0.5) * level).astype(BF16)


def halves():
    core = lax.axis_index("group")
    mine = pl.ds(pl.multiple_of(core * 512, 512), 512)
    other = pl.ds(pl.multiple_of((1 - core) * 512, 512), 512)
    return mine, other


def project_kernel(x_ref, owner_ref, w_hbm, give_ref, keep_ref, restored, weight, sem):
    copy = pltpu.make_async_copy(w_hbm, weight, sem)
    copy.start()
    quantize(x_ref, restored)
    core = lax.axis_index("group")
    n = iota((128, 128), 0)
    half = jnp.where(n < 64, 1 - core, core)
    owner = ((((n & 63) >> 2) * 4 + half + (n & 1) * 2) << 1) + ((n >> 1) & 1)
    chosen = (owner_ref[...] == owner).astype(F32).astype(BF16)
    rows = dot(chosen, restored[...]).astype(BF16)
    copy.wait()
    both = dot(rows, weight[...])
    give_ref[...] = both[0:64]
    keep_ref[...] = both[64:128]


def by24(n):
    return (n * 2731) >> 16


def prepare_kernel(chosen_ref, order_ref):
    a = iota((256, 64), 0)
    e = ((a >> 1) + EP_FIRST) & 127
    chosen = iota((256, 64), 1) == (((e >> 3) << 1) + (e & 1)) * 2 + (a & 1)
    chosen_ref[...] = chosen.astype(F32).astype(BF16)
    a = iota((256, 256), 0)
    source = (((a >> 1) & 7) << 5) + ((a >> 4) << 1) + (a & 1)
    order_ref[...] = (iota((256, 256), 1) == source).astype(F32).astype(BF16)


def spread_kernel(keep_ref, got_ref, chosen_ref, order_ref, out_ref):
    projected = (keep_ref[...] + got_ref[...]).astype(BF16)
    rows = dot(chosen_ref[...], projected).astype(BF16)
    order = order_ref[...]
    for g in range(8):
        part = rows[g * 32 : (g + 1) * 32]
        stack = jnp.concatenate([part[:, f * 128 : (f + 1) * 128] for f in range(8)], axis=0)
        out_ref[pl.ds(g * 256, 256), :] = dot(order, stack).astype(BF16)


def expand_matrix(zp):
    e = (by24(iota((768, 128), 0)) + REGION_FIRST) & 31
    return (iota((768, 128), 1) == ((e & 15) << 3) + zp * 2 + (e >> 4)).astype(BF16)


def item_code(n):
    r = n - by24(n) * 24
    return jnp.where(r < 12, r, r + 4).astype(F32)


def setup_kernel(order_ref, expand_ref):
    a = iota((256, 256), 0)
    order_ref[...] = (iota((256, 256), 1) == ((a & 15) << 4) + (a >> 4)).astype(F32).astype(BF16)
    expand_ref[:, 0:128] = expand_matrix(my_zp())
    taken = item_code(iota((768, 128), 0))
    expand_ref[:, 128:256] = jnp.where(iota((768, 128), 1) == 0, -taken, 0.0).astype(BF16)


def dispatch_kernel(
    own_ref, order_ref, expand_ref, ids_ref, ids_got_ref, send_ref, normed_ref, rows, pick
):
    core = lax.axis_index("group")
    zp = my_zp()
    expert = iota((128, 128), 0)
    earlier = (expert < iota((128, 128), 1)).astype(F32).astype(BF16)
    expand = expand_ref[...]
    ones = jnp.ones((128, 128), BF16)
    for member in range(2):
        k = (zp + 4 - core - 2 * member) & 3
        ids = jnp.where(core == 1, ids_ref[k], ids_got_ref[k])
        named = expert == ids[0:1, :]
        for t in range(1, 8):
            named = named | (expert == ids[t : t + 1, :])
        rank = dot(named.astype(F32).astype(BF16), earlier)
        code = jnp.where(named, rank + 16.0 * member, -1.0)
        normed_ref[pl.ds(member * 128, 128), 1024:1152] = code.T.astype(BF16)
        found = dot(expand, jnp.concatenate([code.astype(BF16), ones], axis=0))
        pick[:, pl.ds(member * 128, 128)] = (found == 0.0).astype(F32).astype(BF16)
    order = order_ref[...]
    for g in range(8):
        slots = (g * 16 + EP_FIRST) % 128
        part = dot(order, own_ref[pl.ds(g * 256, 256), :]).astype(BF16)
        for f in range(8):
            for member in range(2):
                first = (f * 2 + member) * 16
                rows[pl.ds(member * 128 + slots, 16), pl.ds(f * 128, 128)] = part[first : first + 16]
    for member in range(2):
        at = pl.ds(member * 128, 128)
        value = rows[at, :].astype(F32)
        inverse = lax.rsqrt(jnp.mean(value * value, axis=1, keepdims=True) + 1e-06)
        normed_ref[at, 0:1024] = (value * inverse).astype(BF16)
    for part in range(2):
        at = pl.ds(part * 384, 384)
        send_ref[at, :] = dot(pick[at, :], normed_ref[0:256, 0:1024]).astype(BF16)
    normed_ref[256:384, 0:1024] = rows[pl.ds(pl.multiple_of((zp >> 1) * 128, 128), 128), :]


def gate_kernel(normed_ref, router_ref, mix_ref):
    mix_ref[256:384, :] = normed_ref[256:384, 0:1024]
    expand = expand_matrix(my_zp())
    wanted = item_code(iota((128, 768), 1))
    for member in range(2):
        at = pl.ds(member * 128, 128)
        code = normed_ref[at, 1024:1152]
        logits = dot(normed_ref[at, 0:1024], router_ref[...])
        weights = jnp.where(code.astype(F32) >= 0.0, jnp.exp(logits), 0.0)
        gates = weights / jnp.sum(weights, axis=1, keepdims=True)
        found = dot_nt(code, expand)
        spread = dot_nt(gates.astype(BF16), expand)
        mix_ref[at, 0:768] = jnp.where(found == wanted, spread, 0.0).astype(BF16)


def expert_kernel(x_ref, gate_ref, up_ref, down_ref, out_hbm, hidden, stage, sems):
    def act(gate, up):
        return (gate / (1.0 + jnp.exp(-gate)) * up).astype(BF16)

    last = jnp.concatenate([gate_ref[0, :, 256:384], up_ref[0, :, 256:384]], axis=1)
    copies = []
    for i in range(2):
        at = pl.ds(i * 384, 384)
        x = x_ref[at, :]
        hidden[at, 0:256] = act(dot(x, gate_ref[0, :, 0:256]), dot(x, up_ref[0, :, 0:256]))
        both = dot(x, last)
        hidden[at, 256:384] = act(both[:, 0:128], both[:, 128:256])
        stage[at, :] = dot(hidden[at, :], down_ref[0]).astype(BF16)
        for j in range(2):
            rows = pl.ds(i * 384 + j * 192, 192)
            copies.append(
                pltpu.make_async_copy(
                    stage.at[rows, :], out_hbm.at[rows, :], sems.at[i * 2 + j]
                )
            )
            copies[-1].start()
    for copy in copies:
        copy.wait()


def mix_kernel(mix_ref, back_ref, two_ref, one_ref, three_ref, own_ref, total):
    zp = my_zp()
    total[...] = dot(mix_ref[0:256, 0:768], back_ref[...])
    for k, ref in ((2, two_ref), (1, one_ref), (3, three_ref), (0, own_ref)):
        value = total[pl.ds(pl.multiple_of((((zp + k) & 3) >> 1) * 128, 128), 128), :]
        if k == 0:
            value = value + mix_ref[256:384, :].astype(F32)
        ref[...] = value.astype(ref.dtype)


def sum_kernel(whose, own_ref, two_ref, one_ref, three_ref, out_ref):
    lanes = halves()[whose]
    total = own_ref[:, lanes] + two_ref[:, lanes].astype(F32)
    total = total + one_ref[:, lanes].astype(F32)
    out_ref[...] = (total + three_ref[:, lanes].astype(F32)).astype(BF16)


def call(kernel, outs, ins, scratch=(), specs=None, out_spec=VMEM):
    return pl.pallas_call(
        kernel,
        out_shape=[jax.ShapeDtypeStruct(shape, dtype) for shape, dtype in outs],
        in_specs=specs or [VMEM] * len(ins),
        out_specs=[out_spec] * len(outs),
        scratch_shapes=list(scratch),
        compiler_params=PARAMS,
    )(*ins)


def pinned(x):
    return pltpu.with_memory_space_constraint(x, pltpu.HBM)


def further(i, k):
    return (i & ~7) + ((i + 2 * k) & 7)


def send_to(x, pairs):
    return lax.ppermute(x, ("group", "ep"), [(a * 128 + i, b * 128 + j) for (a, i), (b, j) in pairs])


def exchange(x, groups):
    return lax.all_to_all(x, "ep", 0, 0, axis_index_groups=groups, tiled=True)


def body(
    thinker_rows,
    owner_map,
    talker_ids,
    project_weight,
    router_weight,
    expert_gate,
    expert_up,
    expert_down,
):
    chips = range(128)
    give, keep = call(
        project_kernel,
        [((64, 1024), F32)] * 2,
        (pinned(thinker_rows), pinned(owner_map.reshape(1, 128)), pinned(project_weight)),
        [pltpu.VMEM((128, 1024), BF16), pltpu.VMEM((1024, 1024), BF16), pltpu.SemaphoreType.DMA],
        [VMEM, VMEM, HBM],
    )
    got = lax.ppermute(give, "group", SWAP)
    chosen, order = call(prepare_kernel, [((256, 64), BF16), ((256, 256), BF16)], ())
    (sent,) = call(spread_kernel, [((2048, 128), BF16)], (keep, got, chosen, order))
    own_ids = talker_ids.T
    ids = [own_ids]
    for k in (1, 2, 3):
        ids.append(send_to(own_ids, [((1, i), (1, further(i, k))) for i in chips]))
    ids = jnp.stack(ids)
    sent, ids = lax.optimization_barrier((sent, ids))
    own = exchange(sent.reshape(128, 16, 128), EP)
    copies = lax.optimization_barrier(jnp.broadcast_to(ids[None], (64, 4, 8, 128)))
    got_ids = send_to(copies, [((1, i), (0, i)) for i in chips])
    own, got_ids = lax.optimization_barrier((own, got_ids))
    order, expand = call(setup_kernel, [((256, 256), BF16), ((768, 256), BF16)], ())
    send, normed = call(
        dispatch_kernel,
        [((768, 1024), BF16), ((384, 1152), BF16)],
        (own.reshape(2048, 128), order, expand, ids, got_ids[0]),
        [pltpu.VMEM((256, 1024), BF16), pltpu.VMEM((768, 256), BF16)],
    )
    items = exchange(send.reshape(32, 24, 1024), REGIONS)
    (mix,) = call(gate_kernel, [((384, 1024), BF16)], (normed, router_weight))
    (expert_out,) = call(
        expert_kernel,
        [((768, 1024), BF16)],
        (items.reshape(768, 1024), expert_gate, expert_up, expert_down),
        [
            pltpu.VMEM((768, 384), BF16),
            pltpu.VMEM((768, 1024), BF16),
            pltpu.SemaphoreType.DMA((4,)),
        ],
        out_spec=HBM,
    )
    back = exchange(expert_out.reshape(32, 24, 1024), REGIONS)
    two, one, three, total = call(
        mix_kernel,
        [((128, 1024), BF16)] * 3 + [((128, 1024), F32)],
        (mix, back.reshape(768, 1024)),
        [pltpu.VMEM((256, 1024), F32)],
    )
    parts = []
    for k, part in ((1, one), (3, three), (2, two)):
        ends = [(i, further(i, k)) for i in chips]
        parts.append(send_to(part, [((j >> 1 & 1, i), (j >> 1 & 1, j)) for i, j in ends]))
    half = [((128, 512), BF16)]
    (other,) = call(functools.partial(sum_kernel, 1), half, (total, *parts))
    swapped = send_to(other, [((i >> 1 & 1, i), (1 - (i >> 1 & 1), i)) for i in chips])
    (mine,) = call(functools.partial(sum_kernel, 0), half, (total, *parts))
    return jnp.where(lax.axis_index("group") == my_zp() & 1, mine, swapped)


def solution(mesh):
    return jax.shard_map(
        body,
        mesh=mesh,
        in_specs=(
            P("ep", "group"),
            P("ep", None),
            P("ep", None),
            P("group", None),
            P(),
            P("ep", None, None),
            P("ep", None, None),
            P("ep", None, None),
        ),
        out_specs=P("ep", "group"),
        check_vma=False,
    )
```
